512 devices in a mesh: row: 32 (over x, y, core), col: 16 (over z).
Axes of the slice: x: 4, y: 4, z: 16, core: 2. Of those that a mesh axis runs over, the one named last changes fastest.
Arguments:
- features: bfloat16 [65536, 128], P(('row', 'col')), may hold values from -6 to 6
- tile_values: bfloat16 [32, 16, 96, 128, 128], P('row', 'col'), may hold values from -0.109375 to 0.109375
- tile_rows: int32 [32, 16, 96], P('row', 'col'), may hold values from 0 to 15
- tile_cols: int32 [32, 16, 96], P('row', 'col'), may hold values from 0 to 31
- tile_rels: int32 [32, 16, 96], P('row', 'col'), may hold values from 0 to 3
- live: int32 [32, 16], P('row', 'col'), may hold values from 24 to 96, as said below
- weights: bfloat16 [4, 128, 128], replicated, may hold values from -0.25 to 0.25
- bias: float32 [128], replicated, may hold values from -3 to 3
- out_grad: bfloat16 [65536, 128], P(('row', 'col')), may hold values from -6 to 6
Outputs:
- activated: bfloat16 [65536, 128], P(('row', 'col'))
- feature_grad: float32 [65536, 128], P(('row', 'col'))
- weight_grad: float32 [4, 128, 128], replicated
- bias_grad: float32 [128], replicated
The draws below stay inside these ranges and needn't reach their ends.
Inputs may be any that keep to these rules, and one draw needn't show every extreme that they name: Each grid cell uses the first live of its 96 tile slots; some cell uses all 96.
All inputs are finite; a program needn't handle non-finite values.
Results may differ from the reference program's by a relative error of at most 0.008.
Values may be sent and summed in bfloat16 or wider, within the bound.
No kernel may reach another device: no remote copies, remote signals or barrier semaphores. Data moves between devices by JAX's collectives and lax.ppermute only.
A program may use at most 64 MiB of HBM per device.

```python
import jax
import jax.numpy as jnp
from jax import lax

RB = 16
K = 96
FEAT = 128
RELS = 4
NB = 512
CB = 32
N = 65536
N_ROW = 32
N_COL = 16


def draw_live(key, part):
    key = jax.random.fold_in(key, 5)
    first_key, second_key = jax.random.split(key)
    counts = jax.random.randint(first_key, (N_ROW * N_COL,), K // 4, K + 1)
    chosen = jax.random.randint(second_key, (), 0, N_ROW * N_COL)
    counts = jnp.where(jnp.arange(N_ROW * N_COL) == chosen, K, counts)
    return counts.reshape(N_ROW, N_COL).astype(jnp.int32)


def place_ends(entries, rng, least, high):
    spot = [jax.random.randint(jax.random.fold_in(rng, axis), (), 0, length) for axis, length in enumerate(entries.shape)]
    longest = entries.shape.index(max(entries.shape))
    next_to = spot[:longest] + [(spot[longest] + 1) % entries.shape[longest]] + spot[longest + 1:]
    return entries.at[tuple(spot)].set(least).at[tuple(next_to)].set(high)


def level_of(stream_key, shape, cuts, smallest, largest):
    def one(dim, parts):
        heights = jax.random.uniform(jax.random.fold_in(jax.random.fold_in(stream_key, 6), dim), (parts,), jnp.float32, smallest / len(cuts), largest / len(cuts))
        return jnp.repeat(jnp.exp(heights), shape[dim] // parts).reshape((-1,) + (1,) * (len(shape) - dim - 1))

    loudness = one(*cuts[0])
    for cut in cuts[1:]:
        loudness = loudness * one(*cut)
    return loudness


def normal_values(key, extent, deviation, limit, shards=(), held_as=jnp.bfloat16):
    level = level_of(key, extent, shards, -0.22, 0.18) if shards else 1.0
    drawn = jax.random.normal(key, extent, jnp.float32) * deviation * level
    return jnp.minimum(jnp.maximum(drawn, -limit), limit).astype(held_as)


def setup_inputs(seed: int = 0) -> dict:
    splits = jax.random.split(jax.random.key(seed), 10)
    features = normal_values(splits[0], (N, FEAT), 1.0, 6.0, ((0, 512),))
    tile_values = normal_values(splits[1], (N_ROW, N_COL, K, 128, 128), (32 * K * N_COL // RB) ** -0.5, 0.109375, ((0, 32), (1, 16)))
    tile_rows = place_ends(jax.random.randint(splits[2], (N_ROW, N_COL, K), 0, RB), jax.random.fold_in(splits[2], 1), 0, RB - 1).astype(jnp.int32)
    tile_cols = place_ends(jax.random.randint(splits[3], (N_ROW, N_COL, K), 0, CB), jax.random.fold_in(splits[3], 1), 0, CB - 1).astype(jnp.int32)
    tile_rels = place_ends(jax.random.randint(splits[4], (N_ROW, N_COL, K), 0, 4), jax.random.fold_in(splits[4], 1), 0, 3).astype(jnp.int32)
    live = draw_live(jax.random.fold_in(splits[9], 71), 0)
    weights = normal_values(splits[6], (RELS, FEAT, FEAT), 512 ** -0.5, 0.25)
    bias = normal_values(splits[7], (FEAT,), 0.5, 3.0, (), jnp.float32)
    out_grad = normal_values(splits[8], (N, FEAT), 1.0, 6.0, ((0, 512),))
    return dict(features=features, tile_values=tile_values, tile_rows=tile_rows, tile_cols=tile_cols, tile_rels=tile_rels, live=live, weights=weights, bias=bias, out_grad=out_grad)


def silu_slope(z_values):
    sigma = jax.nn.sigmoid(z_values)
    return sigma * (1.0 + z_values * (1.0 - sigma))


def reference(features, tile_values, tile_rows, tile_cols, tile_rels, live, weights, bias, out_grad):
    shard_rows = RB * 128 // N_COL
    col_feats = features.reshape(N_ROW, N_COL, shard_rows, 128).transpose(1, 0, 2, 3).reshape(N_COL, CB, 128, 128)
    slot_range = jnp.arange(K, dtype=jnp.int32)
    cells = jnp.arange(N_ROW * N_COL, dtype=jnp.int32)

    def cell_values(row_group, col_group):
        values = tile_values[row_group, col_group].astype(jnp.float32)
        keeping = (slot_range < live[row_group, col_group]).astype(jnp.float32)
        return values * keeping[:, None, None]

    def forward_cell(carry, cell):
        row_group = cell // N_COL
        col_group = cell % N_COL
        values = cell_values(row_group, col_group)
        picked = col_feats[col_group][tile_cols[row_group, col_group]].astype(jnp.float32)
        products = jnp.einsum("kij,kjf->kif", values, picked, precision=lax.Precision.HIGHEST)
        slot_ids = tile_rels[row_group, col_group] * NB + row_group * RB + tile_rows[row_group, col_group]
        return carry.at[slot_ids].add(products), None

    partial_value = lax.scan(forward_cell, jnp.zeros((4 * NB, 128, 128), jnp.float32), cells)[0]
    partial_value = partial_value.reshape(4, NB * 128, 128)
    wide_weights = weights.astype(jnp.float32)
    z_full = jnp.einsum("rnf,rfg->ng", partial_value, wide_weights, precision=lax.Precision.HIGHEST) + bias
    activated = (z_full * jax.nn.sigmoid(z_full)).astype(jnp.bfloat16)
    grad_z = (out_grad.astype(jnp.float32) * silu_slope(z_full)).astype(jnp.bfloat16)
    grad_wide = grad_z.astype(jnp.float32)
    weight_grad = jnp.einsum("rnf,ng->rfg", partial_value, grad_wide, precision=lax.Precision.HIGHEST)
    bias_grad = jnp.sum(grad_wide, axis=0)
    back_rows = jnp.einsum("ng,rfg->rnf", grad_wide, wide_weights, precision=lax.Precision.HIGHEST).astype(jnp.bfloat16)
    back_rows = back_rows.reshape(4 * NB, 128, 128)

    def backward_cell(carry, cell):
        row_group = cell // N_COL
        col_group = cell % N_COL
        values = cell_values(row_group, col_group)
        slot_ids = tile_rels[row_group, col_group] * NB + row_group * RB + tile_rows[row_group, col_group]
        back_tiles = back_rows[slot_ids].astype(jnp.float32)
        tile_terms = jnp.einsum("kji,kjf->kif", values, back_tiles, precision=lax.Precision.HIGHEST)
        targets = col_group * CB + tile_cols[row_group, col_group]
        return carry.at[targets].add(tile_terms), None

    col_grads = lax.scan(backward_cell, jnp.zeros((N_COL * CB, 128, 128), jnp.float32), cells)[0]
    feature_grad = col_grads.reshape(N_COL, N_ROW, shard_rows, 128).transpose(1, 0, 2, 3).reshape(NB * 128, 128)
    return activated, feature_grad, weight_grad, bias_grad
```

```python
import jax
import jax.numpy as jnp
from jax import lax
from jax.experimental import pallas as pl
from jax.experimental.pallas import tpu as pltpu
from jax.sharding import PartitionSpec as P

RB = 16
CB = 32
RELS = 4
B = 128
STEP = 4
SLICE = CB // RELS
PART = B // SLICE


def dot(a, b):
    return jnp.dot(a, b, preferred_element_type=jnp.float32)


def forward_kernel(rows, cols, rels, live, x, v, w, z, p, acc):
    acc[...] = jnp.zeros_like(acc)
    count = live[0, 0]

    def group(step, carry):
        first = step * STEP
        for u in range(STEP):
            k = first + u
            row = rows[0, 0, k]
            lane = pl.multiple_of(rels[0, 0, k] * B, B)
            product = dot(v[0, 0, k], x[cols[0, 0, k]])
            product = jnp.where(k < count, product, 0.0)
            acc[row, :, pl.ds(lane, B)] += product
        return carry

    lax.fori_loop(0, (count + STEP - 1) // STEP, group, 0)
    wide = w[...]

    def finish(row, carry):
        held = acc[row].astype(jnp.bfloat16)
        p[row] = held
        z[row] = dot(held, wide).astype(jnp.bfloat16)
        return carry

    lax.fori_loop(0, RB, finish, 0, unroll=2)


def middle_kernel(parts, bias, out_grad, activated, grad_t, bias_row):
    z = parts[0].astype(jnp.float32)
    for c in range(1, parts.shape[0]):
        z = z + parts[c].astype(jnp.float32)
    z = z + bias[...]
    s = jax.nn.sigmoid(z)
    activated[...] = (z * s).astype(jnp.bfloat16)
    slope = s * (1.0 + z * (1.0 - s))
    grad = (out_grad[...].astype(jnp.float32) * slope).astype(jnp.bfloat16)
    wide = grad.astype(jnp.float32)
    grad_t[...] = wide.T.astype(jnp.bfloat16)
    total = jnp.sum(wide, axis=0, keepdims=True)
    keep = lax.broadcasted_iota(jnp.int32, (8, B), 0) == 0
    bias_row[...] = jnp.where(keep, total, 0.0)


def backward_kernel(rows, cols, rels, live, grad_t, v, p, w, out, back, acc, wgrad):
    acc[...] = jnp.zeros_like(acc)
    wgrad[...] = jnp.zeros_like(wgrad)
    wide = w[...]
    count = live[0, 0]

    def start(row, carry):
        g = grad_t[row]
        back[row] = dot(wide, g).astype(jnp.bfloat16)
        wgrad[...] += dot(g, p[row])
        return carry

    lax.fori_loop(0, RB, start, 0, unroll=2)

    def group(step, carry):
        first = step * STEP
        for u in range(STEP):
            k = first + u
            at = pl.multiple_of(rels[0, 0, k] * B, B)
            product = dot(back[rows[0, 0, k], pl.ds(at, B), :], v[0, 0, k])
            product = jnp.where(k < count, product, 0.0)
            acc[cols[0, 0, k]] += product
        return carry

    lax.fori_loop(0, (count + STEP - 1) // STEP, group, 0)
    out[:, :B, :] = acc[...].astype(jnp.bfloat16)
    for b in range(CB):
        rel, part = b // SLICE, b % SLICE
        term = wgrad[part * PART : (part + 1) * PART, rel * B : (rel + 1) * B]
        high = term.astype(jnp.bfloat16)
        low = (term - high.astype(jnp.float32)).astype(jnp.bfloat16)
        out[b, B : B + PART, :] = high
        out[b, B + PART : B + 2 * PART, :] = low


VMEM = pl.BlockSpec(memory_space=pltpu.VMEM)
SMEM = pl.BlockSpec(memory_space=pltpu.SMEM)
PARAMS = pltpu.CompilerParams(vmem_limit_bytes=32 * 1024 * 1024)


def copies(block, axis, count):
    wide = jnp.broadcast_to(block[None], (count,) + block.shape)
    return lax.all_to_all(wide, axis, 0, 0, tiled=True)


def on_device(
    features, tile_values, tile_rows, tile_cols, tile_rels, live, weights, bias, out_grad
):
    ncol = RB
    wide_weights = weights.reshape(RELS * B, B)
    blocks = copies(features, "row", CB)
    z_parts, p_wide = pl.pallas_call(
        forward_kernel,
        out_shape=(
            jax.ShapeDtypeStruct((RB, B, B), jnp.bfloat16),
            jax.ShapeDtypeStruct((RB, B, RELS * B), jnp.bfloat16),
        ),
        in_specs=[SMEM] * 4 + [VMEM] * 3,
        out_specs=(VMEM, VMEM),
        scratch_shapes=[pltpu.VMEM((RB, B, RELS * B), jnp.float32)],
        compiler_params=PARAMS,
        name="forward",
    )(tile_rows, tile_cols, tile_rels, live, blocks, tile_values, wide_weights)
    z_parts = lax.all_to_all(z_parts, "col", 0, 0, tiled=True)
    activated, grad_t, bias_row = pl.pallas_call(
        middle_kernel,
        out_shape=(
            jax.ShapeDtypeStruct((B, B), jnp.bfloat16),
            jax.ShapeDtypeStruct((B, B), jnp.bfloat16),
            jax.ShapeDtypeStruct((8, B), jnp.float32),
        ),
        in_specs=[VMEM] * 3,
        out_specs=(VMEM,) * 3,
        compiler_params=PARAMS,
        name="middle",
    )(z_parts, bias.reshape(1, B), out_grad)
    grad_all = lax.all_gather(grad_t, "col", axis=0, tiled=False)
    sent = pl.pallas_call(
        backward_kernel,
        out_shape=jax.ShapeDtypeStruct((CB, B + 2 * PART, B), jnp.bfloat16),
        in_specs=[SMEM] * 4 + [VMEM] * 4,
        out_specs=VMEM,
        scratch_shapes=[
            pltpu.VMEM((RB, RELS * B, B), jnp.bfloat16),
            pltpu.VMEM((CB, B, B), jnp.float32),
            pltpu.VMEM((B, RELS * B), jnp.float32),
        ],
        compiler_params=PARAMS,
        name="backward",
    )(tile_rows, tile_cols, tile_rels, live, grad_all, tile_values, p_wide, wide_weights)
    received = lax.all_to_all(sent, "row", 0, 0, tiled=True)
    summed = jnp.sum(received.astype(jnp.float32), axis=0)
    feature_grad = summed[:B].T
    own = summed[B : B + PART] + summed[B + PART :]
    own = jnp.concatenate([own, bias_row], axis=0)
    own = jnp.sum(copies(own, "col", ncol), axis=0)
    every = copies(own, "row", CB)
    weight_grad = every[:, :PART].reshape(RELS, B, B).transpose(0, 2, 1)
    bias_grad = jnp.sum(every[:, PART], axis=0)
    return (activated, feature_grad, weight_grad, bias_grad)


def solution(mesh):
    placed = (
        P(("row", "col"), None),
        P("row", "col", None, None, None),
        P("row", "col", None),
        P("row", "col", None),
        P("row", "col", None),
        P("row", "col"),
        P(),
        P(),
        P(("row", "col"), None),
    )
    return jax.shard_map(
        on_device,
        mesh=mesh,
        in_specs=placed,
        out_specs=(P(("row", "col"), None), P(("row", "col"), None), P(), P()),
        check_vma=False,
    )
```

```python
import jax
import jax.numpy as jnp
from jax import lax
from jax.experimental import pallas as pl
from jax.experimental.pallas import tpu as pltpu
from jax.sharding import PartitionSpec as P

RB = 16
CB = 32
RELS = 4
B = 128
STEP = 4
SLICE = CB // RELS
PART = B // SLICE


def dot(a, b):
    return jnp.dot(a, b, preferred_element_type=jnp.float32)


def forward_kernel(rows, cols, rels, live, x, v, w, z, p, acc):
    acc[...] = jnp.zeros_like(acc)
    count = live[0, 0]

    def group(step, carry):
        first = step * STEP
        for u in range(STEP):
            k = first + u
            row = rows[0, 0, k]
            lane = pl.multiple_of(rels[0, 0, k] * B, B)
            product = dot(v[0, 0, k], x[cols[0, 0, k]])
            product = jnp.where(k < count, product, 0.0)
            acc[row, :, pl.ds(lane, B)] += product
        return carry

    lax.fori_loop(0, (count + STEP - 1) // STEP, group, 0)
    wide = w[...]

    def finish(row, carry):
        held = acc[row].astype(jnp.bfloat16)
        p[row] = held
        z[row] = dot(held, wide).astype(jnp.bfloat16)
        return carry

    lax.fori_loop(0, RB, finish, 0, unroll=2)


def middle_kernel(parts, bias, out_grad, activated, grad_t):
    z = parts[0].astype(jnp.float32)
    for c in range(1, parts.shape[0]):
        z = z + parts[c].astype(jnp.float32)
    z = z + bias[...]
    s = jax.nn.sigmoid(z)
    activated[...] = (z * s).astype(jnp.bfloat16)
    slope = s * (1.0 + z * (1.0 - s))
    grad = (out_grad[...].astype(jnp.float32) * slope).astype(jnp.bfloat16)
    grad_t[...] = grad.astype(jnp.float32).T.astype(jnp.bfloat16)


def weight_kernel(grad_t, p, out, total):
    total[...] = jnp.zeros_like(total)

    def add(row, carry):
        total[...] += dot(grad_t[row], p[row])
        return carry

    lax.fori_loop(0, RB, add, 0, unroll=2)
    for b in range(CB):
        rel, part = b // SLICE, b % SLICE
        out[b] = total[part * PART : (part + 1) * PART, rel * B : (rel + 1) * B]


def spread_kernel(parts, out):
    total = parts[0]
    for r in range(1, parts.shape[0]):
        total = total + parts[r]
    for c in range(out.shape[0]):
        out[c] = total


def backward_kernel(rows, cols, rels, live, grad_t, v, w, out, bias_sum, back, acc):
    acc[...] = jnp.zeros_like(acc)
    wide = w[...]
    count = live[0, 0]
    ones = jnp.ones((8, B), jnp.bfloat16)
    bias_sum[...] = jnp.zeros_like(bias_sum)

    def start(row, carry):
        g = grad_t[row]
        back[row] = dot(wide, g).astype(jnp.bfloat16)
        bias_sum[...] += lax.dot_general(
            ones, g, (((1,), (1,)), ((), ())), preferred_element_type=jnp.float32
        )
        return carry

    lax.fori_loop(0, RB, start, 0, unroll=2)

    def group(step, carry):
        first = step * STEP
        for u in range(STEP):
            k = first + u
            at = pl.multiple_of(rels[0, 0, k] * B, B)
            product = dot(back[rows[0, 0, k], pl.ds(at, B), :], v[0, 0, k])
            product = jnp.where(k < count, product, 0.0)
            acc[cols[0, 0, k]] += product
        return carry

    lax.fori_loop(0, (count + STEP - 1) // STEP, group, 0)
    out[:, :B, :] = acc[...].astype(jnp.bfloat16)
    out[:, B:, :] = jnp.zeros((CB, 2 * PART, B), jnp.bfloat16)


def append_kernel(sent, parts, bias_sum, out):
    total = parts[0]
    for c in range(1, parts.shape[0]):
        total = total + parts[c]
    row = lax.broadcasted_iota(jnp.int32, (PART, B), 0)
    term = jnp.broadcast_to(bias_sum[0:1, :], (PART, B))
    high = term.astype(jnp.bfloat16).astype(jnp.float32)
    pair = jnp.where(row == 0, high, jnp.where(row == 1, term - high, 0.0))
    both = jnp.concatenate([total, pair], axis=0).astype(jnp.bfloat16)
    for r in range(CB):
        out[r, B:, :] = both


VMEM = pl.BlockSpec(memory_space=pltpu.VMEM)
SMEM = pl.BlockSpec(memory_space=pltpu.SMEM)
PARAMS = pltpu.CompilerParams(vmem_limit_bytes=32 * 1024 * 1024)


def swap(blocks, axis):
    return lax.all_to_all(blocks, axis, 0, 0, tiled=True)


def on_device(
    features, tile_values, tile_rows, tile_cols, tile_rels, live, weights, bias, out_grad
):
    ids = (tile_rows, tile_cols, tile_rels, live)
    wide_weights = weights.reshape(RELS * B, B)
    blocks = swap(jnp.broadcast_to(features[None], (CB, B, B)), "row")
    z_parts, p_wide = pl.pallas_call(
        forward_kernel,
        out_shape=(
            jax.ShapeDtypeStruct((RB, B, B), jnp.bfloat16),
            jax.ShapeDtypeStruct((RB, B, RELS * B), jnp.bfloat16),
        ),
        in_specs=[SMEM] * 4 + [VMEM] * 3,
        out_specs=(VMEM, VMEM),
        scratch_shapes=[pltpu.VMEM((RB, B, RELS * B), jnp.float32)],
        compiler_params=PARAMS,
        name="forward",
    )(*ids, blocks, tile_values, wide_weights)
    activated, grad_t = pl.pallas_call(
        middle_kernel,
        out_shape=(
            jax.ShapeDtypeStruct((B, B), jnp.bfloat16),
            jax.ShapeDtypeStruct((B, B), jnp.bfloat16),
        ),
        in_specs=[VMEM] * 3,
        out_specs=(VMEM,) * 2,
        compiler_params=PARAMS,
        name="middle",
    )(swap(z_parts, "col"), bias.reshape(1, B), out_grad)
    grad_all = lax.all_gather(grad_t, "col", axis=0, tiled=False)
    weight_parts = pl.pallas_call(
        weight_kernel,
        out_shape=jax.ShapeDtypeStruct((CB, PART, B), jnp.float32),
        in_specs=[VMEM] * 2,
        out_specs=VMEM,
        scratch_shapes=[pltpu.VMEM((B, RELS * B), jnp.float32)],
        compiler_params=PARAMS,
        name="weight",
    )(grad_all, p_wide)
    own = pl.pallas_call(
        spread_kernel,
        out_shape=jax.ShapeDtypeStruct((RB, PART, B), jnp.float32),
        in_specs=[VMEM],
        out_specs=VMEM,
        compiler_params=PARAMS,
        name="spread",
    )(swap(weight_parts, "row"))
    own = swap(own, "col")
    sent, bias_sum = pl.pallas_call(
        backward_kernel,
        out_shape=(
            jax.ShapeDtypeStruct((CB, B + 2 * PART, B), jnp.bfloat16),
            jax.ShapeDtypeStruct((8, B), jnp.float32),
        ),
        in_specs=[SMEM] * 4 + [VMEM] * 3,
        out_specs=(VMEM, VMEM),
        scratch_shapes=[
            pltpu.VMEM((RB, RELS * B, B), jnp.bfloat16),
            pltpu.VMEM((CB, B, B), jnp.float32),
        ],
        compiler_params=PARAMS,
        cost_estimate=pl.CostEstimate(flops=10**9, bytes_accessed=10**7, transcendentals=0),
        name="backward",
    )(*ids, grad_all, tile_values, wide_weights)
    sent = pl.pallas_call(
        append_kernel,
        out_shape=jax.ShapeDtypeStruct(sent.shape, sent.dtype),
        in_specs=[VMEM] * 3,
        out_specs=VMEM,
        input_output_aliases={0: 0},
        compiler_params=PARAMS,
        name="append",
    )(sent, own, bias_sum)
    received = swap(sent, "row")
    feature_grad = jnp.sum(received[:, :B].astype(jnp.float32), axis=0).T
    every = received[:, B : B + PART].astype(jnp.float32)
    weight_grad = every.reshape(RELS, B, B).transpose(0, 2, 1)
    bias_grad = jnp.sum(received[:, B + PART : B + PART + 2].astype(jnp.float32), axis=(0, 1))
    return (activated, feature_grad, weight_grad, bias_grad)


def solution(mesh):
    placed = (
        P(("row", "col"), None),
        P("row", "col", None, None, None),
        P("row", "col", None),
        P("row", "col", None),
        P("row", "col", None),
        P("row", "col"),
        P(),
        P(),
        P(("row", "col"), None),
    )
    return jax.shard_map(
        on_device,
        mesh=mesh,
        in_specs=placed,
        out_specs=(P(("row", "col"), None), P(("row", "col"), None), P(), P()),
        check_vma=False,
    )
```

```python
import jax
import jax.numpy as jnp
from jax import lax
from jax.experimental import pallas as pl
from jax.experimental.pallas import tpu as pltpu
from jax.sharding import PartitionSpec as P

RB = 16
CB = 32
RELS = 4
B = 128
STEP = 24
TILES = 96
BATCH = 4
GROUPS = TILES // STEP
SLICE = CB // RELS
PART = B // SLICE


def dot(a, b):
    return jnp.dot(a, b, preferred_element_type=jnp.float32)


def place(ids, k):
    code = ids[0, 0, k]
    row, col = code & (RB - 1), (code >> 4) & (CB - 1)
    return row, col, pl.multiple_of((code >> 9) * B, B)


def forward_kernel(ids, live, core, own_x, other_x, v, w, z, p, x, acc, tiles, wide, sems):
    def chunk(g):
        span = pl.ds(g * STEP, STEP)
        return pltpu.make_async_copy(v.at[0, 0, span], tiles.at[span], sems.at[g])

    load_w = pltpu.make_async_copy(w, wide, sems.at[GROUPS])
    for g in range(GROUPS):
        chunk(g).start()
    load_w.start()
    acc[...] = jnp.zeros_like(acc)
    x[0] = own_x[...]
    x[1] = other_x[...]
    count = live[0, 0]
    mine = core[0, 0]

    def group(g, carry):
        chunk(g).wait()
        first = g * STEP

        @pl.when(first < count)
        def _():
            for u in range(STEP):
                k = first + u
                row, col, lane = place(ids, k)
                product = dot(tiles[k], x[(col & 1) ^ mine, col >> 1])
                product = jnp.where(k < count, product, 0.0)
                acc[row, :, pl.ds(lane, B)] += product

        return carry

    lax.fori_loop(0, GROUPS, group, 0)
    load_w.wait()

    def finish(i, carry):
        rows = pl.ds(i * BATCH, BATCH)
        held = acc[rows].astype(jnp.bfloat16)
        p[rows] = held
        part = dot(held.reshape(BATCH * B, RELS * B), wide[...])
        z[rows] = part.astype(jnp.bfloat16).reshape(BATCH, B, B)
        return carry

    lax.fori_loop(0, RB // BATCH, finish, 0, unroll=2)


def middle_kernel(parts, bias, out_grad, activated, grad_t):
    z = parts[0].astype(jnp.float32)
    for c in range(1, parts.shape[0]):
        z = z + parts[c].astype(jnp.float32)
    z = z + bias[...]
    s = jax.nn.sigmoid(z)
    activated[...] = (z * s).astype(jnp.bfloat16)
    slope = s * (1.0 + z * (1.0 - s))
    grad = (out_grad[...].astype(jnp.float32) * slope).astype(jnp.bfloat16)
    grad_t[...] = grad.astype(jnp.float32).T.astype(jnp.bfloat16)


def weight_kernel(grad_t, p, out, total):
    total[...] = jnp.zeros_like(total)

    def add(i, carry):
        g = jnp.concatenate([grad_t[2 * i], grad_t[2 * i + 1]], axis=1)
        total[...] += dot(g, p[pl.ds(2 * i, 2)].reshape(2 * B, RELS * B))
        return carry

    lax.fori_loop(0, RB // 2, add, 0, unroll=2)
    for b in range(CB):
        rel, part = b // SLICE, b % SLICE
        out[b] = total[part * PART : (part + 1) * PART, rel * B : (rel + 1) * B]


def spread_kernel(parts, out):
    total = parts[0]
    for r in range(1, parts.shape[0]):
        total = total + parts[r]
    total = total.astype(jnp.bfloat16)
    for c in range(out.shape[0]):
        out[c] = total


def backward_kernel(
    ids, live, core, grad_t, v, w, kept, given, bias_sum, back, acc, tiles, sems
):
    def chunk(g):
        span = pl.ds(g * STEP, STEP)
        return pltpu.make_async_copy(v.at[0, 0, span], tiles.at[span], sems.at[g])

    for g in range(GROUPS):
        chunk(g).start()
    acc[...] = jnp.zeros_like(acc)
    wide = w[...]
    count = live[0, 0]
    mine = core[0, 0]
    ones = jnp.ones((8, 2 * B), jnp.bfloat16)
    bias_sum[...] = jnp.zeros_like(bias_sum)

    def start(i, carry):
        g = jnp.concatenate([grad_t[2 * i], grad_t[2 * i + 1]], axis=1)
        both = dot(wide, g).astype(jnp.bfloat16)
        back[2 * i] = both[:, :B]
        back[2 * i + 1] = both[:, B:]
        bias_sum[...] += lax.dot_general(
            ones, g, (((1,), (1,)), ((), ())), preferred_element_type=jnp.float32
        )
        return carry

    lax.fori_loop(0, RB // 2, start, 0, unroll=2)

    def group(g, carry):
        chunk(g).wait()
        first = g * STEP

        @pl.when(first < count)
        def _():
            for u in range(STEP):
                k = first + u
                row, col, at = place(ids, k)
                product = dot(back[row, pl.ds(at, B), :], tiles[k])
                product = jnp.where(k < count, product, 0.0)
                acc[(col & 1) ^ mine, col >> 1] += product

        return carry

    lax.fori_loop(0, GROUPS, group, 0)
    kept[...] = acc[0].astype(jnp.bfloat16)
    given[...] = acc[1].astype(jnp.bfloat16)


def join_kernel(kept, taken, out):
    total = kept[...].astype(jnp.float32) + taken[...].astype(jnp.float32)
    out[:, :B, :] = total.astype(jnp.bfloat16)
    out[:, B:, :] = jnp.zeros((out.shape[0], 3 * PART, B), jnp.bfloat16)


def total_kernel(parts, bias_sum, out):
    total = parts[0].astype(jnp.float32)
    for c in range(1, parts.shape[0]):
        total = total + parts[c].astype(jnp.float32)
    out[:PART] = total.astype(jnp.bfloat16)
    row = lax.broadcasted_iota(jnp.int32, (PART, B), 0)
    term = jnp.broadcast_to(bias_sum[0:1, :], (PART, B))
    high = term.astype(jnp.bfloat16).astype(jnp.float32)
    pair = jnp.where(row == 0, high, jnp.where(row == 1, term - high, 0.0))
    out[PART:] = pair.astype(jnp.bfloat16)


def append_kernel(core, sent, own, other, out):
    first = core[0, 0] == 0
    mine = own[...].astype(jnp.float32)
    theirs = other[...].astype(jnp.float32)
    low = jnp.where(first, mine, theirs)
    high = jnp.where(first, theirs, mine)
    row = lax.broadcasted_iota(jnp.int32, (PART, B), 0)
    second = jnp.concatenate([high[PART + 8 :], high[PART : PART + 8]], axis=0)
    pair = jnp.where(row < 8, low[PART:], second)
    rows = jnp.concatenate([low[:PART], high[:PART], pair], axis=0).astype(jnp.bfloat16)
    for r in range(out.shape[0]):
        out[r, B:, :] = rows


def final_kernel(received, feature_grad, weight_grad, bias_grad):
    total = received[0, :B].astype(jnp.float32)
    pair = received[0, B + 2 * PART :].astype(jnp.float32)
    for r in range(1, received.shape[0]):
        total = total + received[r, :B].astype(jnp.float32)
        pair = pair + received[r, B + 2 * PART :].astype(jnp.float32)
    feature_grad[...] = total.T
    bias_grad[...] = jnp.sum(pair, axis=0, keepdims=True)
    each = SLICE // 2
    for rel in range(RELS):
        parts = [received[rel * each + i, B : B + 2 * PART] for i in range(each)]
        weight_grad[rel] = jnp.concatenate(parts, axis=0).astype(jnp.float32).T


VMEM = pl.BlockSpec(memory_space=pltpu.VMEM)
SMEM = pl.BlockSpec(memory_space=pltpu.SMEM)
ANY = pl.BlockSpec(memory_space=pl.ANY)
WIDE = pltpu.CompilerParams(vmem_limit_bytes=48 * 1024 * 1024)
PARAMS = pltpu.CompilerParams(vmem_limit_bytes=32 * 1024 * 1024)


def swap(blocks, axis, groups=None):
    return lax.all_to_all(blocks, axis, 0, 0, tiled=True, axis_index_groups=groups)


def other_core(block):
    return lax.ppermute(block, "row", [(r, r ^ 1) for r in range(CB)])


def on_device(
    features, tile_values, tile_rows, tile_cols, tile_rels, live, weights, bias, out_grad
):
    ids = tile_rows + (tile_cols << 4) + (tile_rels << 9)
    wide_weights = weights.reshape(RELS * B, B)
    chips = CB // 2
    same_core = [[2 * chip + core for chip in range(chips)] for core in range(2)]
    core = jnp.reshape(lax.axis_index("row") % 2, (1, 1)).astype(jnp.int32)
    own_x = swap(jnp.broadcast_to(features[None], (chips, B, B)), "row", same_core)
    other_x = other_core(own_x)
    z_parts, p_wide = pl.pallas_call(
        forward_kernel,
        out_shape=(
            jax.ShapeDtypeStruct((RB, B, B), jnp.bfloat16),
            jax.ShapeDtypeStruct((RB, B, RELS * B), jnp.bfloat16),
        ),
        in_specs=[SMEM] * 3 + [VMEM] * 2 + [ANY] * 2,
        out_specs=(VMEM, VMEM),
        scratch_shapes=[
            pltpu.VMEM((2, chips, B, B), jnp.bfloat16),
            pltpu.VMEM((RB, B, RELS * B), jnp.float32),
            pltpu.VMEM((TILES, B, B), jnp.bfloat16),
            pltpu.VMEM((RELS * B, B), jnp.bfloat16),
            pltpu.SemaphoreType.DMA((GROUPS + 1,)),
        ],
        compiler_params=WIDE,
        name="forward",
    )(ids, live, core, own_x, other_x, tile_values, wide_weights)
    activated, grad_t = pl.pallas_call(
        middle_kernel,
        out_shape=(
            jax.ShapeDtypeStruct((B, B), jnp.bfloat16),
            jax.ShapeDtypeStruct((B, B), jnp.bfloat16),
        ),
        in_specs=[VMEM] * 3,
        out_specs=(VMEM,) * 2,
        compiler_params=PARAMS,
        name="middle",
    )(swap(z_parts, "col"), bias.reshape(1, B), out_grad)
    grad_all = lax.all_gather(grad_t, "col", axis=0, tiled=False)
    weight_parts = pl.pallas_call(
        weight_kernel,
        out_shape=jax.ShapeDtypeStruct((CB, PART, B), jnp.float32),
        in_specs=[VMEM] * 2,
        out_specs=VMEM,
        scratch_shapes=[pltpu.VMEM((B, RELS * B), jnp.float32)],
        compiler_params=PARAMS,
        name="weight",
    )(grad_all, p_wide)
    weight_parts = swap(weight_parts, "row")
    kept, given, bias_sum = pl.pallas_call(
        backward_kernel,
        out_shape=(
            jax.ShapeDtypeStruct((chips, B, B), jnp.bfloat16),
            jax.ShapeDtypeStruct((chips, B, B), jnp.bfloat16),
            jax.ShapeDtypeStruct((8, B), jnp.float32),
        ),
        in_specs=[SMEM] * 3 + [VMEM, ANY, VMEM],
        out_specs=(VMEM,) * 3,
        scratch_shapes=[
            pltpu.VMEM((RB, RELS * B, B), jnp.bfloat16),
            pltpu.VMEM((2, chips, B, B), jnp.float32),
            pltpu.VMEM((TILES, B, B), jnp.bfloat16),
            pltpu.SemaphoreType.DMA((GROUPS,)),
        ],
        compiler_params=PARAMS,
        cost_estimate=pl.CostEstimate(flops=10**9, bytes_accessed=10**7, transcendentals=0),
        name="backward",
    )(ids, live, core, grad_all, tile_values, wide_weights)
    taken = other_core(given)
    own = pl.pallas_call(
        spread_kernel,
        out_shape=jax.ShapeDtypeStruct((RB, PART, B), jnp.bfloat16),
        in_specs=[VMEM],
        out_specs=VMEM,
        compiler_params=PARAMS,
        name="spread",
    )(weight_parts)
    own = swap(own, "col")
    sent = pl.pallas_call(
        join_kernel,
        out_shape=jax.ShapeDtypeStruct((chips, B + 3 * PART, B), jnp.bfloat16),
        in_specs=[VMEM] * 2,
        out_specs=VMEM,
        compiler_params=PARAMS,
        cost_estimate=pl.CostEstimate(flops=10**6, bytes_accessed=10**6, transcendentals=0),
        name="join",
    )(kept, taken)
    own = pl.pallas_call(
        total_kernel,
        out_shape=jax.ShapeDtypeStruct((2 * PART, B), jnp.bfloat16),
        in_specs=[VMEM] * 2,
        out_specs=VMEM,
        compiler_params=PARAMS,
        name="total",
    )(own, bias_sum)
    sent = pl.pallas_call(
        append_kernel,
        out_shape=jax.ShapeDtypeStruct(sent.shape, sent.dtype),
        in_specs=[SMEM] + [VMEM] * 3,
        out_specs=VMEM,
        input_output_aliases={1: 0},
        compiler_params=PARAMS,
        name="append",
    )(core, sent, own, other_core(own))
    feature_grad, weight_grad, bias_grad = pl.pallas_call(
        final_kernel,
        out_shape=(
            jax.ShapeDtypeStruct((B, B), jnp.float32),
            jax.ShapeDtypeStruct((RELS, B, B), jnp.float32),
            jax.ShapeDtypeStruct((1, B), jnp.float32),
        ),
        in_specs=[VMEM],
        out_specs=(VMEM,) * 3,
        compiler_params=PARAMS,
        name="final",
    )(swap(sent, "row", same_core))
    return (activated, feature_grad, weight_grad, bias_grad.reshape(B))


def solution(mesh):
    placed = (
        P(("row", "col"), None),
        P("row", "col", None, None, None),
        P("row", "col", None),
        P("row", "col", None),
        P("row", "col", None),
        P("row", "col"),
        P(),
        P(),
        P(("row", "col"), None),
    )
    return jax.shard_map(
        on_device,
        mesh=mesh,
        in_specs=placed,
        out_specs=(P(("row", "col"), None), P(("row", "col"), None), P(), P()),
        check_vma=False,
    )
```

```python
import functools

import jax
import jax.numpy as jnp
from jax import lax
from jax.experimental import pallas as pl
from jax.experimental.pallas import tpu as pltpu
from jax.sharding import PartitionSpec as P

RB = 16
CB = 32
RELS = 4
B = 128
STEP = 24
TILES = 96
BATCH = 4
SHORT = 16
GROUPS = TILES // STEP
SLICE = CB // RELS
PART = B // SLICE


def dot(a, b):
    return jnp.dot(a, b, preferred_element_type=jnp.float32)


def place(code):
    row, col, rel = code & (RB - 1), (code >> 4) & (CB - 1), (code >> 9) & (RELS - 1)
    return row, col, pl.multiple_of(rel * B, B)


def forward_kernel(
    which, ids, live, side, core, own_x, other_x, v, w, z, p, x, acc, tiles, wide, listed, sems
):
    def chunk(g):
        span = pl.ds(g * STEP, STEP)
        return pltpu.make_async_copy(v.at[0, 0, span], tiles.at[span], sems.at[g])

    load_w = pltpu.make_async_copy(w, wide, sems.at[GROUPS])
    for g in range(GROUPS):
        chunk(g).start()
    load_w.start()
    acc[...] = jnp.zeros_like(acc)
    x[0] = own_x[...]
    x[1] = other_x[...]
    mine = core[0, 0]
    wanted = side[0, 0] ^ which

    def put(k, at):
        code = ids[0, 0, k]
        listed[at] = code + (k << 11)
        return at + jnp.where((code & 1) == wanted, 1, 0)

    count = lax.fori_loop(0, live[0, 0], put, 0)
    for u in range(SHORT):
        listed[count + u] = 0
    for g in range(GROUPS):
        chunk(g).wait()

    def group(g, carry):
        for u in range(SHORT):
            i = g * SHORT + u
            code = listed[i]
            row, col, lane = place(code)
            product = dot(tiles[code >> 11], x[(col & 1) ^ mine, col >> 1])
            product = jnp.where(i < count, product, 0.0)
            acc[row >> 1, :, pl.ds(lane, B)] += product
        return carry

    lax.fori_loop(0, (count + SHORT - 1) // SHORT, group, 0)
    load_w.wait()

    def finish(i, carry):
        rows = pl.ds(i * BATCH, BATCH)
        held = acc[rows].astype(jnp.bfloat16)
        p[rows] = held
        part = dot(held.reshape(BATCH * B, RELS * B), wide[...])
        z[rows] = part.astype(z.dtype).reshape(BATCH, B, B)
        return carry

    lax.fori_loop(0, RB // 2 // BATCH, finish, 0, unroll=2)


def middle_kernel(parts, bias, out_grad, activated, grad_t):
    z = parts[0].astype(jnp.float32)
    for c in range(1, parts.shape[0]):
        z = z + parts[c].astype(jnp.float32)
    z = z + bias[...]
    s = jax.nn.sigmoid(z)
    activated[...] = (z * s).astype(jnp.bfloat16)
    slope = s * (1.0 + z * (1.0 - s))
    grad = (out_grad[...].astype(jnp.float32) * slope).astype(jnp.bfloat16)
    grad_t[...] = grad.astype(jnp.float32).T.astype(jnp.bfloat16)


def weight_kernel(side, grad_t, p_own, p_other, out, total):
    total[...] = jnp.zeros_like(total)
    mine = side[0, 0]

    def add(i, carry):
        g = jnp.concatenate([grad_t[2 * i + mine], grad_t[2 * i + 1 - mine]], axis=1)
        total[...] += dot(g, jnp.concatenate([p_own[i], p_other[i]], axis=0))
        return carry

    lax.fori_loop(0, RB // 2, add, 0, unroll=2)
    for b in range(CB):
        rel, part = b // SLICE, b % SLICE
        out[b] = total[part * PART : (part + 1) * PART, rel * B : (rel + 1) * B]


def spread_kernel(parts, out):
    total = parts[0]
    for r in range(1, parts.shape[0]):
        total = total + parts[r]
    total = total.astype(jnp.bfloat16)
    for c in range(out.shape[0]):
        out[c] = total


def backward_kernel(
    ids, live, core, grad_t, v, w, kept, given, bias_sum, back, acc
):
    acc[...] = jnp.zeros_like(acc)
    wide = w[...]
    count = live[0, 0]
    mine = core[0, 0]
    ones = jnp.ones((8, 2 * B), jnp.bfloat16)
    bias_sum[...] = jnp.zeros_like(bias_sum)

    def start(i, carry):
        g = jnp.concatenate([grad_t[2 * i], grad_t[2 * i + 1]], axis=1)
        both = dot(wide, g).astype(jnp.bfloat16)
        back[2 * i] = both[:, :B]
        back[2 * i + 1] = both[:, B:]
        bias_sum[...] += lax.dot_general(
            ones, g, (((1,), (1,)), ((), ())), preferred_element_type=jnp.float32
        )
        return carry

    lax.fori_loop(0, RB // 2, start, 0, unroll=2)

    def group(g, carry):
        first = g * STEP

        @pl.when(first < count)
        def _():
            for u in range(STEP):
                k = first + u
                row, col, at = place(ids[0, 0, k])
                product = dot(back[row, pl.ds(at, B), :], v[0, 0, k])
                product = jnp.where(k < count, product, 0.0)
                acc[(col & 1) ^ mine, col >> 1] += product

        return carry

    lax.fori_loop(0, GROUPS, group, 0)
    kept[...] = acc[0].astype(jnp.bfloat16)
    given[...] = acc[1].astype(jnp.bfloat16)


def join_kernel(kept, taken, out):
    total = kept[...].astype(jnp.float32) + taken[...].astype(jnp.float32)
    out[:, :B, :] = total.astype(jnp.bfloat16)
    out[:, B:, :] = jnp.zeros((out.shape[0], 3 * PART, B), jnp.bfloat16)


def total_kernel(parts, bias_sum, out):
    total = parts[0].astype(jnp.float32)
    for c in range(1, parts.shape[0]):
        total = total + parts[c].astype(jnp.float32)
    out[:PART] = total.astype(jnp.bfloat16)
    row = lax.broadcasted_iota(jnp.int32, (PART, B), 0)
    term = jnp.broadcast_to(bias_sum[0:1, :], (PART, B))
    high = term.astype(jnp.bfloat16).astype(jnp.float32)
    pair = jnp.where(row == 0, high, jnp.where(row == 1, term - high, 0.0))
    out[PART:] = pair.astype(jnp.bfloat16)


def append_kernel(core, sent, own, other, out):
    first = core[0, 0] == 0
    mine = own[...].astype(jnp.float32)
    theirs = other[...].astype(jnp.float32)
    low = jnp.where(first, mine, theirs)
    high = jnp.where(first, theirs, mine)
    row = lax.broadcasted_iota(jnp.int32, (PART, B), 0)
    second = jnp.concatenate([high[PART + 8 :], high[PART : PART + 8]], axis=0)
    pair = jnp.where(row < 8, low[PART:], second)
    rows = jnp.concatenate([low[:PART], high[:PART], pair], axis=0).astype(jnp.bfloat16)
    for r in range(out.shape[0]):
        out[r, B:, :] = rows


def final_kernel(received, feature_grad, weight_grad, bias_grad):
    total = received[0, :B].astype(jnp.float32)
    pair = received[0, B + 2 * PART :].astype(jnp.float32)
    for r in range(1, received.shape[0]):
        total = total + received[r, :B].astype(jnp.float32)
        pair = pair + received[r, B + 2 * PART :].astype(jnp.float32)
    feature_grad[...] = total.T
    bias_grad[...] = jnp.sum(pair, axis=0, keepdims=True)
    each = SLICE // 2
    for rel in range(RELS):
        parts = [received[rel * each + i, B : B + 2 * PART] for i in range(each)]
        weight_grad[rel] = jnp.concatenate(parts, axis=0).astype(jnp.float32).T


VMEM = pl.BlockSpec(memory_space=pltpu.VMEM)
SMEM = pl.BlockSpec(memory_space=pltpu.SMEM)
ANY = pl.BlockSpec(memory_space=pl.ANY)
WIDE = pltpu.CompilerParams(vmem_limit_bytes=50 * 1024 * 1024)
PARAMS = pltpu.CompilerParams(vmem_limit_bytes=32 * 1024 * 1024)


def swap(blocks, axis, groups=None):
    return lax.all_to_all(blocks, axis, 0, 0, tiled=True, axis_index_groups=groups)


def other_core(block):
    return lax.ppermute(block, "row", [(r, r ^ 1) for r in range(CB)])


def on_device(
    features, tile_values, tile_rows, tile_cols, tile_rels, live, weights, bias, out_grad
):
    ids = tile_rows + (tile_cols << 4) + (tile_rels << 9)
    wide_weights = weights.reshape(RELS * B, B)
    chips = CB // 2
    same_core = [[2 * chip + core for chip in range(chips)] for core in range(2)]
    core = jnp.reshape(lax.axis_index("row") % 2, (1, 1)).astype(jnp.int32)
    own_x = swap(jnp.broadcast_to(features[None], (chips, B, B)), "row", same_core)
    other_x = other_core(own_x)
    side = jnp.reshape(lax.axis_index("col") % 2, (1, 1)).astype(jnp.int32)

    def forward(which, z_type):
        return pl.pallas_call(
            functools.partial(forward_kernel, which),
            out_shape=(
                jax.ShapeDtypeStruct((RB // 2, B, B), z_type),
                jax.ShapeDtypeStruct((RB // 2, B, RELS * B), jnp.bfloat16),
            ),
            in_specs=[SMEM] * 4 + [VMEM] * 2 + [ANY] * 2,
            out_specs=(VMEM, VMEM),
            scratch_shapes=[
                pltpu.VMEM((2, chips, B, B), jnp.bfloat16),
                pltpu.VMEM((RB // 2, B, RELS * B), jnp.float32),
                pltpu.VMEM((TILES, B, B), jnp.bfloat16),
                pltpu.VMEM((RELS * B, B), jnp.bfloat16),
                pltpu.SMEM((TILES + SHORT,), jnp.int32),
                pltpu.SemaphoreType.DMA((GROUPS + 1,)),
            ],
            compiler_params=WIDE,
            cost_estimate=pl.CostEstimate(flops=10**9, bytes_accessed=10**7, transcendentals=0),
            name="forward",
        )(ids, live, side, core, own_x, other_x, tile_values, wide_weights)

    def partner(r, c):
        return c ^ 1 if r % 2 == 0 else ((c + 1) ^ 1) - 1

    pairs = [(r * RB + c, r * RB + partner(r, c) % RB) for r in range(CB) for c in range(RB)]
    z_other, p_other = forward(1, jnp.bfloat16)
    z_other = lax.ppermute(z_other, ("row", "col"), pairs)
    z_own, p_own = forward(0, jnp.float32)
    z_parts = (z_own + z_other.astype(jnp.float32)).astype(jnp.bfloat16)
    same_side = [[2 * i + c for i in range(RB // 2)] for c in range(2)]
    activated, grad_t = pl.pallas_call(
        middle_kernel,
        out_shape=(
            jax.ShapeDtypeStruct((B, B), jnp.bfloat16),
            jax.ShapeDtypeStruct((B, B), jnp.bfloat16),
        ),
        in_specs=[VMEM] * 3,
        out_specs=(VMEM,) * 2,
        compiler_params=PARAMS,
        name="middle",
    )(swap(z_parts, "col", same_side), bias.reshape(1, B), out_grad)
    grad_all = lax.all_gather(grad_t, "col", axis=0, tiled=False)
    weight_parts = pl.pallas_call(
        weight_kernel,
        out_shape=jax.ShapeDtypeStruct((CB, PART, B), jnp.float32),
        in_specs=[SMEM] + [VMEM] * 3,
        out_specs=VMEM,
        scratch_shapes=[pltpu.VMEM((B, RELS * B), jnp.float32)],
        compiler_params=PARAMS,
        name="weight",
    )(side, grad_all, p_own, p_other)
    weight_parts = swap(weight_parts, "row")
    kept, given, bias_sum = pl.pallas_call(
        backward_kernel,
        out_shape=(
            jax.ShapeDtypeStruct((chips, B, B), jnp.bfloat16),
            jax.ShapeDtypeStruct((chips, B, B), jnp.bfloat16),
            jax.ShapeDtypeStruct((8, B), jnp.float32),
        ),
        in_specs=[SMEM] * 3 + [VMEM] * 3,
        out_specs=(VMEM,) * 3,
        scratch_shapes=[
            pltpu.VMEM((RB, RELS * B, B), jnp.bfloat16),
            pltpu.VMEM((2, chips, B, B), jnp.float32),
        ],
        compiler_params=PARAMS,
        cost_estimate=pl.CostEstimate(flops=10**9, bytes_accessed=10**7, transcendentals=0),
        name="backward",
    )(ids, live, core, grad_all, tile_values, wide_weights)
    taken = other_core(given)
    own = pl.pallas_call(
        spread_kernel,
        out_shape=jax.ShapeDtypeStruct((RB, PART, B), jnp.bfloat16),
        in_specs=[VMEM],
        out_specs=VMEM,
        compiler_params=PARAMS,
        name="spread",
    )(weight_parts)
    own = swap(own, "col")
    sent = pl.pallas_call(
        join_kernel,
        out_shape=jax.ShapeDtypeStruct((chips, B + 3 * PART, B), jnp.bfloat16),
        in_specs=[VMEM] * 2,
        out_specs=VMEM,
        compiler_params=PARAMS,
        cost_estimate=pl.CostEstimate(flops=10**6, bytes_accessed=10**6, transcendentals=0),
        name="join",
    )(kept, taken)
    own = pl.pallas_call(
        total_kernel,
        out_shape=jax.ShapeDtypeStruct((2 * PART, B), jnp.bfloat16),
        in_specs=[VMEM] * 2,
        out_specs=VMEM,
        compiler_params=PARAMS,
        name="total",
    )(own, bias_sum)
    sent = pl.pallas_call(
        append_kernel,
        out_shape=jax.ShapeDtypeStruct(sent.shape, sent.dtype),
        in_specs=[SMEM] + [VMEM] * 3,
        out_specs=VMEM,
        input_output_aliases={1: 0},
        compiler_params=PARAMS,
        name="append",
    )(core, sent, own, other_core(own))
    feature_grad, weight_grad, bias_grad = pl.pallas_call(
        final_kernel,
        out_shape=(
            jax.ShapeDtypeStruct((B, B), jnp.float32),
            jax.ShapeDtypeStruct((RELS, B, B), jnp.float32),
            jax.ShapeDtypeStruct((1, B), jnp.float32),
        ),
        in_specs=[VMEM],
        out_specs=(VMEM,) * 3,
        compiler_params=PARAMS,
        name="final",
    )(swap(sent, "row", same_core))
    return (activated, feature_grad, weight_grad, bias_grad.reshape(B))


def solution(mesh):
    placed = (
        P(("row", "col"), None),
        P("row", "col", None, None, None),
        P("row", "col", None),
        P("row", "col", None),
        P("row", "col", None),
        P("row", "col"),
        P(),
        P(),
        P(("row", "col"), None),
    )
    return jax.shard_map(
        on_device,
        mesh=mesh,
        in_specs=placed,
        out_specs=(P(("row", "col"), None), P(("row", "col"), None), P(), P()),
        check_vma=False,
    )
```

```python
import functools

import jax
import jax.numpy as jnp
from jax import lax
from jax.experimental import pallas as pl
from jax.experimental.pallas import tpu as pltpu
from jax.sharding import PartitionSpec as P

RB = 16
CB = 32
RELS = 4
B = 128
TILES = 96
BATCH = 4
SHORT = 16
CHUNK_BITS = 4
CHUNK = 1 << CHUNK_BITS
CHUNKS = TILES // CHUNK
SLICE = CB // RELS
PART = B // SLICE


def dot(a, b):
    return jnp.dot(a, b, preferred_element_type=jnp.float32)


def place(code):
    row, col, rel = code & (RB - 1), (code >> 4) & (CB - 1), (code >> 9) & (RELS - 1)
    return row, col, pl.multiple_of(rel * B, B)


def forward_kernel(
    which, ids, live, side, core, own_x, other_x, v, w, z, p, *rest
):
    lists = rest[0] if which == 0 else None
    x, acc, tiles, wide, listed, sems = rest[-6:]

    def chunk(g):
        span = pl.ds(g * CHUNK, CHUNK)
        return pltpu.make_async_copy(v.at[0, 0, span], tiles.at[span], sems.at[g])

    load_w = pltpu.make_async_copy(w.at[: RELS * B], wide, sems.at[CHUNKS])
    for g in range(CHUNKS):
        chunk(g).start()
    load_w.start()
    acc[...] = jnp.zeros_like(acc)
    x[0] = own_x[...]
    x[1] = other_x[...]
    mine = core[0, 0]
    wanted = side[0, 0] ^ which

    def put(k, at):
        code = ids[0, 0, k]
        listed[at] = code + (k << 11)
        return at + jnp.where((code & 1) == wanted, 1, 0)

    count = lax.fori_loop(0, live[0, 0], put, 0)
    for u in range(SHORT):
        listed[count + u] = 0

    def arrive(g, carry):
        chunk(g).wait()
        return carry

    def group(g, arrived):
        last = jnp.minimum(g * SHORT + SHORT, count) - 1
        needed = jnp.maximum((listed[last] >> (11 + CHUNK_BITS)) + 1, arrived)
        lax.fori_loop(arrived, needed, arrive, 0)
        for u in range(SHORT):
            i = g * SHORT + u
            code = listed[i]
            row, col, lane = place(code)
            product = dot(tiles[code >> 11], x[(col & 1) ^ mine, col >> 1])
            product = jnp.where(i < count, product, 0.0)
            acc[row >> 1, :, pl.ds(lane, B)] += product
        return needed

    arrived = lax.fori_loop(0, (count + SHORT - 1) // SHORT, group, 0)
    lax.fori_loop(arrived, CHUNKS, arrive, 0)
    load_w.wait()

    def finish(i, carry):
        rows = pl.ds(i * BATCH, BATCH)
        held = acc[rows].astype(jnp.bfloat16)
        p[rows] = held
        part = dot(held.reshape(BATCH * B, RELS * B), wide[...])
        z[rows] = part.astype(z.dtype).reshape(BATCH, B, B)
        return carry

    lax.fori_loop(0, RB // 2 // BATCH, finish, 0, unroll=2)
    if which == 0:
        both_lists(ids, live[0, 0], side[0, 0], lists)


def both_lists(ids, live, side, lists):
    def put(k, at):
        code = ids[0, 0, k]
        other = (code & 1) ^ side
        lists[other, jnp.where(other == 1, at, k - at)] = code + (k << 11)
        return at + other

    given = lax.fori_loop(0, live, put, 0)
    for u in range(SHORT):
        lists[0, live - given + u] = 0
        lists[1, given + u] = 0
    lists[0, TILES + SHORT] = live - given
    lists[1, TILES + SHORT] = given


def middle_kernel(parts, bias, out_grad, activated, grad_t):
    z = parts[0].astype(jnp.float32)
    for c in range(1, parts.shape[0]):
        z = z + parts[c].astype(jnp.float32)
    z = z + bias[...]
    s = jax.nn.sigmoid(z)
    activated[...] = (z * s).astype(jnp.bfloat16)
    slope = s * (1.0 + z * (1.0 - s))
    grad = (out_grad[...].astype(jnp.float32) * slope).astype(jnp.bfloat16)
    turned = grad.astype(jnp.float32).T.astype(jnp.bfloat16)
    for i in range(grad_t.shape[0]):
        grad_t[i] = turned


def early_kernel(lists, core, grad_t, p, v, w, total, bias_sum, acc, back):
    total[...] = jnp.zeros_like(total)
    bias_sum[...] = jnp.zeros_like(bias_sum)
    acc[...] = jnp.zeros_like(acc)
    weight_rows(grad_t, p, total, bias_sum)
    back_rows(grad_t, w[...], back)
    back_tiles(0, lists, core[0, 0], v, back, acc)


def back_tiles(which, lists, mine, v, back, acc):
    count = lists[which, TILES + SHORT]

    def group(g, carry):
        for u in range(SHORT):
            i = g * SHORT + u
            code = lists[which, i]
            row, col, at = place(code)
            product = dot(back[row >> 1, pl.ds(at, B), :], v[0, 0, code >> 11])
            product = jnp.where(i < count, product, 0.0)
            acc[(col & 1) ^ mine, col >> 1] += product
        return carry

    lax.fori_loop(0, (count + SHORT - 1) // SHORT, group, 0)


def weight_rows(grad_t, p, total, bias_sum):
    ones = jnp.ones((8, 2 * B), jnp.bfloat16)

    def add(i, carry):
        g = jnp.concatenate([grad_t[2 * i], grad_t[2 * i + 1]], axis=1)
        total[...] += dot(g, p[pl.ds(2 * i, 2)].reshape(2 * B, RELS * B))
        bias_sum[...] += lax.dot_general(
            ones, g, (((1,), (1,)), ((), ())), preferred_element_type=jnp.float32
        )
        return carry

    lax.fori_loop(0, RB // 4, add, 0, unroll=2)


def back_rows(grad_t, wide, back):
    def start(i, carry):
        g = jnp.concatenate([grad_t[2 * i], grad_t[2 * i + 1]], axis=1)
        both = dot(wide, g).astype(jnp.bfloat16)
        back[2 * i] = both[:, :B]
        back[2 * i + 1] = both[:, B:]
        return carry

    lax.fori_loop(0, RB // 4, start, 0, unroll=2)


def weight_kernel(grad_t, p, early_total, early_bias, out, bias_sum, total):
    total[...] = early_total[...]
    bias_sum[...] = early_bias[...]
    weight_rows(grad_t, p, total, bias_sum)
    for b in range(CB):
        rel, part = b // SLICE, b % SLICE
        out[b] = total[part * PART : (part + 1) * PART, rel * B : (rel + 1) * B]


def spread_kernel(parts, out):
    total = parts[0]
    for r in range(1, parts.shape[0]):
        total = total + parts[r]
    total = total.astype(jnp.bfloat16)
    for c in range(out.shape[0]):
        out[c] = total


def backward_kernel(lists, core, grad_t, early_acc, v, w, kept, given, back, acc):
    acc[...] = early_acc[...]
    back_rows(grad_t, w[...], back)
    back_tiles(1, lists, core[0, 0], v, back, acc)
    kept[...] = acc[0].astype(jnp.bfloat16)
    given[...] = acc[1].astype(jnp.bfloat16)


def join_kernel(kept, taken, out):
    total = kept[...].astype(jnp.float32) + taken[...].astype(jnp.float32)
    out[:, :B, :] = total.astype(jnp.bfloat16)
    out[:, B:, :] = jnp.zeros((out.shape[0], 3 * PART, B), jnp.bfloat16)


def total_kernel(parts, bias_sum, out):
    total = parts[0].astype(jnp.float32)
    for c in range(1, parts.shape[0]):
        total = total + parts[c].astype(jnp.float32)
    out[:PART] = total.astype(jnp.bfloat16)
    row = lax.broadcasted_iota(jnp.int32, (PART, B), 0)
    term = jnp.broadcast_to(bias_sum[0:1, :], (PART, B))
    high = term.astype(jnp.bfloat16).astype(jnp.float32)
    pair = jnp.where(row == 0, high, jnp.where(row == 1, term - high, 0.0))
    out[PART:] = pair.astype(jnp.bfloat16)


def append_kernel(core, sent, own, other, out):
    first = core[0, 0] == 0
    mine = own[...].astype(jnp.float32)
    theirs = other[...].astype(jnp.float32)
    low = jnp.where(first, mine, theirs)
    high = jnp.where(first, theirs, mine)
    row = lax.broadcasted_iota(jnp.int32, (PART, B), 0)
    second = jnp.concatenate([high[PART + 8 :], high[PART : PART + 8]], axis=0)
    pair = jnp.where(row < 8, low[PART:], second)
    rows = jnp.concatenate([low[:PART], high[:PART], pair], axis=0).astype(jnp.bfloat16)
    for r in range(out.shape[0]):
        out[r, B:, :] = rows


def final_kernel(received, feature_grad, weight_grad, bias_grad):
    total = received[0, :B].astype(jnp.float32)
    pair = received[0, B + 2 * PART :].astype(jnp.float32)
    for r in range(1, received.shape[0]):
        total = total + received[r, :B].astype(jnp.float32)
        pair = pair + received[r, B + 2 * PART :].astype(jnp.float32)
    feature_grad[...] = total.T
    bias_grad[...] = jnp.sum(pair, axis=0, keepdims=True)
    each = SLICE // 2
    for rel in range(RELS):
        parts = [received[rel * each + i, B : B + 2 * PART] for i in range(each)]
        weight_grad[rel] = jnp.concatenate(parts, axis=0).astype(jnp.float32).T


VMEM = pl.BlockSpec(memory_space=pltpu.VMEM)
SMEM = pl.BlockSpec(memory_space=pltpu.SMEM)
ANY = pl.BlockSpec(memory_space=pl.ANY)
WIDE = pltpu.CompilerParams(vmem_limit_bytes=50 * 1024 * 1024)
PARAMS = pltpu.CompilerParams(vmem_limit_bytes=32 * 1024 * 1024)


def swap(blocks, axis, groups=None):
    return lax.all_to_all(blocks, axis, 0, 0, tiled=True, axis_index_groups=groups)


def other_core(block):
    return lax.ppermute(block, "row", [(r, r ^ 1) for r in range(CB)])


def on_device(
    features, tile_values, tile_rows, tile_cols, tile_rels, live, weights, bias, out_grad
):
    ids = tile_rows + (tile_cols << 4) + (tile_rels << 9)
    wide_weights = weights.reshape(RELS * B, B)
    chips = CB // 2
    same_core = [[2 * chip + core for chip in range(chips)] for core in range(2)]
    core = jnp.reshape(lax.axis_index("row") % 2, (1, 1)).astype(jnp.int32)
    own_x = swap(jnp.broadcast_to(features[None], (chips, B, B)), "row", same_core)
    other_x = other_core(own_x)
    side = jnp.reshape(lax.axis_index("col") % 2, (1, 1)).astype(jnp.int32)

    early_weights = jnp.pad(wide_weights, ((0, PART), (0, 0)))

    def forward(which, z_type):
        return pl.pallas_call(
            functools.partial(forward_kernel, which),
            out_shape=(
                jax.ShapeDtypeStruct((RB // 2, B, B), z_type),
                jax.ShapeDtypeStruct((RB // 2, B, RELS * B), jnp.bfloat16),
            )
            + (jax.ShapeDtypeStruct((2, TILES + SHORT + 1), jnp.int32),) * (1 - which),
            in_specs=[SMEM] * 4 + [VMEM] * 2 + [ANY] * 2,
            out_specs=(VMEM, VMEM) + (SMEM,) * (1 - which),
            scratch_shapes=[
                pltpu.VMEM((2, chips, B, B), jnp.bfloat16),
                pltpu.VMEM((RB // 2, B, RELS * B), jnp.float32),
                pltpu.VMEM((TILES, B, B), jnp.bfloat16),
                pltpu.VMEM((RELS * B, B), jnp.bfloat16),
                pltpu.SMEM((TILES + SHORT,), jnp.int32),
                pltpu.SemaphoreType.DMA((CHUNKS + 1,)),
            ],
            compiler_params=WIDE,
            cost_estimate=pl.CostEstimate(flops=10**9, bytes_accessed=10**7, transcendentals=0),
            name="forward",
        )(ids, live, side, core, own_x, other_x, tile_values, early_weights)

    def partner(r, c):
        return c ^ 1 if r % 2 == 0 else ((c + 1) ^ 1) - 1

    pairs = [(r * RB + c, r * RB + partner(r, c) % RB) for r in range(CB) for c in range(RB)]
    z_other, p_other = forward(1, jnp.bfloat16)
    z_other = lax.ppermute(z_other, ("row", "col"), pairs)
    z_own, p_own, lists = forward(0, jnp.float32)
    z_parts = (z_own + z_other.astype(jnp.float32)).astype(jnp.bfloat16)
    same_side = [[2 * i + c for i in range(RB // 2)] for c in range(2)]
    activated, grad_t = pl.pallas_call(
        middle_kernel,
        out_shape=(
            jax.ShapeDtypeStruct((B, B), jnp.bfloat16),
            jax.ShapeDtypeStruct((RB // 2, B, B), jnp.bfloat16),
        ),
        in_specs=[VMEM] * 3,
        out_specs=(VMEM,) * 2,
        compiler_params=PARAMS,
        name="middle",
    )(swap(z_parts, "col", same_side), bias.reshape(1, B), out_grad)
    grad_own = swap(grad_t, "col", same_side)
    grad_other = lax.ppermute(grad_own, ("row", "col"), pairs)
    early_total, early_bias, early_acc = pl.pallas_call(
        early_kernel,
        out_shape=(
            jax.ShapeDtypeStruct((B, RELS * B), jnp.float32),
            jax.ShapeDtypeStruct((8, B), jnp.float32),
            jax.ShapeDtypeStruct((2, chips, B, B), jnp.float32),
        ),
        in_specs=[SMEM] * 2 + [VMEM] * 4,
        out_specs=(VMEM,) * 3,
        scratch_shapes=[pltpu.VMEM((RB // 2, RELS * B, B), jnp.bfloat16)],
        compiler_params=PARAMS,
        cost_estimate=pl.CostEstimate(flops=10**9, bytes_accessed=10**7, transcendentals=0),
        name="early",
    )(lists, core, grad_own, p_own, tile_values, wide_weights)
    weight_parts, bias_sum = pl.pallas_call(
        weight_kernel,
        out_shape=(
            jax.ShapeDtypeStruct((CB, PART, B), jnp.float32),
            jax.ShapeDtypeStruct((8, B), jnp.float32),
        ),
        in_specs=[VMEM] * 4,
        out_specs=(VMEM, VMEM),
        scratch_shapes=[pltpu.VMEM((B, RELS * B), jnp.float32)],
        compiler_params=PARAMS,
        name="weight",
    )(grad_other, p_other, early_total, early_bias)
    weight_parts = swap(weight_parts, "row")
    kept, given = pl.pallas_call(
        backward_kernel,
        out_shape=(
            jax.ShapeDtypeStruct((chips, B, B), jnp.bfloat16),
            jax.ShapeDtypeStruct((chips, B, B), jnp.bfloat16),
        ),
        in_specs=[SMEM] * 2 + [VMEM] * 4,
        out_specs=(VMEM,) * 2,
        scratch_shapes=[
            pltpu.VMEM((RB // 2, RELS * B, B), jnp.bfloat16),
            pltpu.VMEM((2, chips, B, B), jnp.float32),
        ],
        compiler_params=PARAMS,
        cost_estimate=pl.CostEstimate(flops=10**9, bytes_accessed=10**7, transcendentals=0),
        name="backward",
    )(lists, core, grad_other, early_acc, tile_values, wide_weights)
    taken = other_core(given)
    own = pl.pallas_call(
        spread_kernel,
        out_shape=jax.ShapeDtypeStruct((RB, PART, B), jnp.bfloat16),
        in_specs=[VMEM],
        out_specs=VMEM,
        compiler_params=PARAMS,
        name="spread",
    )(weight_parts)
    own = swap(own, "col")
    sent = pl.pallas_call(
        join_kernel,
        out_shape=jax.ShapeDtypeStruct((chips, B + 3 * PART, B), jnp.bfloat16),
        in_specs=[VMEM] * 2,
        out_specs=VMEM,
        compiler_params=PARAMS,
        cost_estimate=pl.CostEstimate(flops=10**6, bytes_accessed=10**6, transcendentals=0),
        name="join",
    )(kept, taken)
    own = pl.pallas_call(
        total_kernel,
        out_shape=jax.ShapeDtypeStruct((2 * PART, B), jnp.bfloat16),
        in_specs=[VMEM] * 2,
        out_specs=VMEM,
        compiler_params=PARAMS,
        name="total",
    )(own, bias_sum)
    sent = pl.pallas_call(
        append_kernel,
        out_shape=jax.ShapeDtypeStruct(sent.shape, sent.dtype),
        in_specs=[SMEM] + [VMEM] * 3,
        out_specs=VMEM,
        input_output_aliases={1: 0},
        compiler_params=PARAMS,
        name="append",
    )(core, sent, own, other_core(own))
    feature_grad, weight_grad, bias_grad = pl.pallas_call(
        final_kernel,
        out_shape=(
            jax.ShapeDtypeStruct((B, B), jnp.float32),
            jax.ShapeDtypeStruct((RELS, B, B), jnp.float32),
            jax.ShapeDtypeStruct((1, B), jnp.float32),
        ),
        in_specs=[VMEM],
        out_specs=(VMEM,) * 3,
        compiler_params=PARAMS,
        name="final",
    )(swap(sent, "row", same_core))
    return (activated, feature_grad, weight_grad, bias_grad.reshape(B))


def solution(mesh):
    placed = (
        P(("row", "col"), None),
        P("row", "col", None, None, None),
        P("row", "col", None),
        P("row", "col", None),
        P("row", "col", None),
        P("row", "col"),
        P(),
        P(),
        P(("row", "col"), None),
    )
    return jax.shard_map(
        on_device,
        mesh=mesh,
        in_specs=placed,
        out_specs=(P(("row", "col"), None), P(("row", "col"), None), P(), P()),
        check_vma=False,
    )
```

```python
import functools

import jax
import jax.numpy as jnp
from jax import lax
from jax.experimental import pallas as pl
from jax.experimental.pallas import tpu as pltpu
from jax.sharding import PartitionSpec as P

RB = 16
CB = 32
RELS = 4
B = 128
TILES = 96
BATCH = 4
SHORT = 16
CHUNK_BITS = 4
CHUNK = 1 << CHUNK_BITS
CHUNKS = TILES // CHUNK
SLICE = CB // RELS
PART = B // SLICE


def dot(a, b):
    return jnp.dot(a, b, preferred_element_type=jnp.float32)


def place(code):
    row, col, rel = code & (RB - 1), (code >> 4) & (CB - 1), (code >> 9) & (RELS - 1)
    return row, col, pl.multiple_of(rel * B, B)


def forward_kernel(
    which, ids, live, side, core, own_x, other_x, v, w, z, p, *rest
):
    lists = rest[0] if which == 0 else None
    x, acc, tiles, wide, listed, sems = rest[-6:]

    def chunk(g):
        span = pl.ds(g * CHUNK, CHUNK)
        return pltpu.make_async_copy(v.at[0, 0, span], tiles.at[span], sems.at[g])

    load_w = pltpu.make_async_copy(w.at[: RELS * B], wide, sems.at[CHUNKS])
    for g in range(CHUNKS):
        chunk(g).start()
    load_w.start()
    acc[...] = jnp.zeros_like(acc)
    x[0] = own_x[...]
    x[1] = other_x[...]
    mine = core[0, 0]
    wanted = side[0, 0] ^ which

    def put(k, at):
        code = ids[0, 0, k]
        listed[at] = code + (k << 11)
        return at + jnp.where((code & 1) == wanted, 1, 0)

    count = lax.fori_loop(0, live[0, 0], put, 0)
    for u in range(SHORT):
        listed[count + u] = 0

    def arrive(g, carry):
        chunk(g).wait()
        return carry

    def group(g, arrived):
        last = jnp.minimum(g * SHORT + SHORT, count) - 1
        needed = jnp.maximum((listed[last] >> (11 + CHUNK_BITS)) + 1, arrived)
        lax.fori_loop(arrived, needed, arrive, 0)
        for u in range(SHORT):
            i = g * SHORT + u
            code = listed[i]
            row, col, lane = place(code)
            product = dot(tiles[code >> 11], x[(col & 1) ^ mine, col >> 1])
            product = jnp.where(i < count, product, 0.0)
            acc[row >> 1, :, pl.ds(lane, B)] += product
        return needed

    arrived = lax.fori_loop(0, (count + SHORT - 1) // SHORT, group, 0)
    lax.fori_loop(arrived, CHUNKS, arrive, 0)
    load_w.wait()

    def finish(i, carry):
        rows = pl.ds(i * BATCH, BATCH)
        held = acc[rows].astype(jnp.bfloat16)
        p[rows] = held
        part = dot(held.reshape(BATCH * B, RELS * B), wide[...])
        z[rows] = part.astype(z.dtype).reshape(BATCH, B, B)
        return carry

    lax.fori_loop(0, RB // 2 // BATCH, finish, 0, unroll=2)
    if which == 0:
        both_lists(ids, live[0, 0], side[0, 0], lists)


def both_lists(ids, live, side, lists):
    def put(k, at):
        code = ids[0, 0, k]
        other = (code & 1) ^ side
        lists[other, jnp.where(other == 1, at, k - at)] = code + (k << 11)
        return at + other

    given = lax.fori_loop(0, live, put, 0)
    for u in range(SHORT):
        lists[0, live - given + u] = 0
        lists[1, given + u] = 0
    lists[0, TILES + SHORT] = live - given
    lists[1, TILES + SHORT] = given


def middle_kernel(parts, bias, out_grad, activated, grad_t):
    z = parts[0].astype(jnp.float32)
    for c in range(1, parts.shape[0]):
        z = z + parts[c].astype(jnp.float32)
    z = z + bias[...]
    s = jax.nn.sigmoid(z)
    activated[...] = (z * s).astype(jnp.bfloat16)
    slope = s * (1.0 + z * (1.0 - s))
    grad = (out_grad[...].astype(jnp.float32) * slope).astype(jnp.bfloat16)
    turned = grad.astype(jnp.float32).T.astype(jnp.bfloat16)
    for i in range(grad_t.shape[0]):
        grad_t[i] = turned


def early_kernel(lists, core, grad_t, p, v, w, total, bias_sum, acc, back):
    total[...] = jnp.zeros_like(total)
    bias_sum[...] = jnp.zeros_like(bias_sum)
    acc[...] = jnp.zeros_like(acc)
    weight_rows(grad_t, p, total, bias_sum)
    back_rows(grad_t, w[...], back)
    back_tiles(0, lists, core[0, 0], v, back, acc)


def back_tiles(which, lists, mine, v, back, acc):
    count = lists[which, TILES + SHORT]

    def group(g, carry):
        for u in range(SHORT):
            i = g * SHORT + u
            code = lists[which, i]
            row, col, at = place(code)
            product = dot(back[row >> 1, pl.ds(at, B), :], v[0, 0, code >> 11])
            product = jnp.where(i < count, product, 0.0)
            acc[(col & 1) ^ mine, col >> 1] += product
        return carry

    lax.fori_loop(0, (count + SHORT - 1) // SHORT, group, 0)


def weight_rows(grad_t, p, total, bias_sum):
    ones = jnp.ones((8, 2 * B), jnp.bfloat16)

    def add(i, carry):
        g = jnp.concatenate([grad_t[2 * i], grad_t[2 * i + 1]], axis=1)
        total[...] += dot(g, p[pl.ds(2 * i, 2)].reshape(2 * B, RELS * B))
        bias_sum[...] += lax.dot_general(
            ones, g, (((1,), (1,)), ((), ())), preferred_element_type=jnp.float32
        )
        return carry

    lax.fori_loop(0, RB // 4, add, 0, unroll=2)


def back_rows(grad_t, wide, back):
    def start(i, carry):
        g = jnp.concatenate([grad_t[2 * i], grad_t[2 * i + 1]], axis=1)
        both = dot(wide, g).astype(jnp.bfloat16)
        back[2 * i] = both[:, :B]
        back[2 * i + 1] = both[:, B:]
        return carry

    lax.fori_loop(0, RB // 4, start, 0, unroll=2)


def spread_kernel(parts, out):
    total = parts[0]
    for r in range(1, parts.shape[0]):
        total = total + parts[r]
    total = total.astype(jnp.bfloat16)
    for c in range(out.shape[0]):
        out[c] = total


def late_kernel(
    lists, core, grad_t, p, v, w, early_total, early_bias, early_acc,
    weight_parts, bias_sum, kept, given, total, back, acc
):
    total[...] = early_total[...]
    bias_sum[...] = early_bias[...]
    weight_rows(grad_t, p, total, bias_sum)
    for b in range(CB):
        rel, part = b // SLICE, b % SLICE
        weight_parts[b] = total[part * PART : (part + 1) * PART, rel * B : (rel + 1) * B]
    acc[...] = early_acc[...]
    back_rows(grad_t, w[...], back)
    back_tiles(1, lists, core[0, 0], v, back, acc)
    kept[...] = acc[0].astype(jnp.bfloat16)
    given[: CB // 2] = acc[1].astype(jnp.bfloat16)
    given[CB // 2] = jnp.zeros((B, B), jnp.bfloat16)


def total_kernel(given, parts, bias_sum, out):
    total = parts[0].astype(jnp.float32)
    for c in range(1, parts.shape[0]):
        total = total + parts[c].astype(jnp.float32)
    row = lax.broadcasted_iota(jnp.int32, (PART, B), 0)
    term = jnp.broadcast_to(bias_sum[0:1, :], (PART, B))
    high = term.astype(jnp.bfloat16).astype(jnp.float32)
    pair = jnp.where(row == 0, high, jnp.where(row == 1, term - high, 0.0))
    out[CB // 2, : 2 * PART, :] = jnp.concatenate([total, pair], axis=0).astype(jnp.bfloat16)


def join_kernel(core, kept, given, taken, out):
    chips = out.shape[0]
    total = kept[...].astype(jnp.float32) + taken[:chips].astype(jnp.float32)
    out[:, :B, :] = total.astype(jnp.bfloat16)
    first = core[0, 0] == 0
    mine = given[chips, : 2 * PART, :].astype(jnp.float32)
    theirs = taken[chips, : 2 * PART, :].astype(jnp.float32)
    low = jnp.where(first, mine, theirs)
    high = jnp.where(first, theirs, mine)
    row = lax.broadcasted_iota(jnp.int32, (PART, B), 0)
    second = jnp.concatenate([high[PART + 8 :], high[PART : PART + 8]], axis=0)
    pair = jnp.where(row < 8, low[PART:], second)
    rows = jnp.concatenate([low[:PART], high[:PART], pair], axis=0).astype(jnp.bfloat16)
    for r in range(chips):
        out[r, B:, :] = rows


def final_kernel(received, feature_grad, weight_grad, bias_grad):
    total = received[0, :B].astype(jnp.float32)
    pair = received[0, B + 2 * PART :].astype(jnp.float32)
    for r in range(1, received.shape[0]):
        total = total + received[r, :B].astype(jnp.float32)
        pair = pair + received[r, B + 2 * PART :].astype(jnp.float32)
    feature_grad[...] = total.T
    bias_grad[...] = jnp.sum(pair, axis=0, keepdims=True)
    each = SLICE // 2
    for rel in range(RELS):
        parts = [received[rel * each + i, B : B + 2 * PART] for i in range(each)]
        weight_grad[rel] = jnp.concatenate(parts, axis=0).astype(jnp.float32).T


VMEM = pl.BlockSpec(memory_space=pltpu.VMEM)
SMEM = pl.BlockSpec(memory_space=pltpu.SMEM)
ANY = pl.BlockSpec(memory_space=pl.ANY)
WIDE = pltpu.CompilerParams(vmem_limit_bytes=50 * 1024 * 1024)
PARAMS = pltpu.CompilerParams(vmem_limit_bytes=32 * 1024 * 1024)


def swap(blocks, axis, groups=None):
    return lax.all_to_all(blocks, axis, 0, 0, tiled=True, axis_index_groups=groups)


def other_core(block):
    return lax.ppermute(block, "row", [(r, r ^ 1) for r in range(CB)])


def on_device(
    features, tile_values, tile_rows, tile_cols, tile_rels, live, weights, bias, out_grad
):
    ids = tile_rows + (tile_cols << 4) + (tile_rels << 9)
    wide_weights = weights.reshape(RELS * B, B)
    chips = CB // 2
    same_core = [[2 * chip + core for chip in range(chips)] for core in range(2)]
    core = jnp.reshape(lax.axis_index("row") & 1, (1, 1)).astype(jnp.int32)
    own_x = swap(jnp.broadcast_to(features[None], (chips, B, B)), "row", same_core)
    other_x = other_core(own_x)
    side = jnp.reshape(lax.axis_index("col") & 1, (1, 1)).astype(jnp.int32)

    early_weights = jnp.pad(wide_weights, ((0, PART), (0, 0)))

    def forward(which, z_type):
        return pl.pallas_call(
            functools.partial(forward_kernel, which),
            out_shape=(
                jax.ShapeDtypeStruct((RB // 2, B, B), z_type),
                jax.ShapeDtypeStruct((RB // 2, B, RELS * B), jnp.bfloat16),
            )
            + (jax.ShapeDtypeStruct((2, TILES + SHORT + 1), jnp.int32),) * (1 - which),
            in_specs=[SMEM] * 4 + [VMEM] * 2 + [ANY] * 2,
            out_specs=(VMEM, VMEM) + (SMEM,) * (1 - which),
            scratch_shapes=[
                pltpu.VMEM((2, chips, B, B), jnp.bfloat16),
                pltpu.VMEM((RB // 2, B, RELS * B), jnp.float32),
                pltpu.VMEM((TILES, B, B), jnp.bfloat16),
                pltpu.VMEM((RELS * B, B), jnp.bfloat16),
                pltpu.SMEM((TILES + SHORT,), jnp.int32),
                pltpu.SemaphoreType.DMA((CHUNKS + 1,)),
            ],
            compiler_params=WIDE,
            cost_estimate=pl.CostEstimate(flops=10**9, bytes_accessed=10**7, transcendentals=0),
            name="forward",
        )(ids, live, side, core, own_x, other_x, tile_values, early_weights)

    def partner(r, c):
        return c ^ 1 if r % 2 == 0 else ((c + 1) ^ 1) - 1

    pairs = [(r * RB + c, r * RB + partner(r, c) % RB) for r in range(CB) for c in range(RB)]
    z_other, p_other = forward(1, jnp.bfloat16)
    z_other = lax.ppermute(z_other, ("row", "col"), pairs)
    z_own, p_own, lists = forward(0, jnp.float32)
    z_parts = (z_own + z_other.astype(jnp.float32)).astype(jnp.bfloat16)
    same_side = [[2 * i + c for i in range(RB // 2)] for c in range(2)]
    activated, grad_t = pl.pallas_call(
        middle_kernel,
        out_shape=(
            jax.ShapeDtypeStruct((B, B), jnp.bfloat16),
            jax.ShapeDtypeStruct((RB // 2, B, B), jnp.bfloat16),
        ),
        in_specs=[VMEM] * 3,
        out_specs=(VMEM,) * 2,
        compiler_params=PARAMS,
        name="middle",
    )(swap(z_parts, "col", same_side), bias.reshape(1, B), out_grad)
    grad_own = swap(grad_t, "col", same_side)
    grad_other = lax.ppermute(grad_own, ("row", "col"), pairs)
    early_total, early_bias, early_acc = pl.pallas_call(
        early_kernel,
        out_shape=(
            jax.ShapeDtypeStruct((B, RELS * B), jnp.float32),
            jax.ShapeDtypeStruct((8, B), jnp.float32),
            jax.ShapeDtypeStruct((2, chips, B, B), jnp.float32),
        ),
        in_specs=[SMEM] * 2 + [VMEM] * 4,
        out_specs=(VMEM,) * 3,
        scratch_shapes=[pltpu.VMEM((RB // 2, RELS * B, B), jnp.bfloat16)],
        compiler_params=PARAMS,
        cost_estimate=pl.CostEstimate(flops=10**9, bytes_accessed=10**7, transcendentals=0),
        name="early",
    )(lists, core, grad_own, p_own, tile_values, wide_weights)
    weight_parts, bias_sum, kept, given = pl.pallas_call(
        late_kernel,
        out_shape=(
            jax.ShapeDtypeStruct((CB, PART, B), jnp.float32),
            jax.ShapeDtypeStruct((8, B), jnp.float32),
            jax.ShapeDtypeStruct((chips, B, B), jnp.bfloat16),
            jax.ShapeDtypeStruct((chips + 1, B, B), jnp.bfloat16),
        ),
        in_specs=[SMEM] * 2 + [VMEM] * 7,
        out_specs=(VMEM,) * 4,
        scratch_shapes=[
            pltpu.VMEM((B, RELS * B), jnp.float32),
            pltpu.VMEM((RB // 2, RELS * B, B), jnp.bfloat16),
            pltpu.VMEM((2, chips, B, B), jnp.float32),
        ],
        compiler_params=PARAMS,
        name="late",
    )(lists, core, grad_other, p_other, tile_values, wide_weights, early_total, early_bias, early_acc)
    own = pl.pallas_call(
        spread_kernel,
        out_shape=jax.ShapeDtypeStruct((RB, PART, B), jnp.bfloat16),
        in_specs=[VMEM],
        out_specs=VMEM,
        compiler_params=PARAMS,
        name="spread",
    )(swap(weight_parts, "row"))
    given = pl.pallas_call(
        total_kernel,
        out_shape=jax.ShapeDtypeStruct(given.shape, given.dtype),
        in_specs=[VMEM] * 3,
        out_specs=VMEM,
        input_output_aliases={0: 0},
        compiler_params=PARAMS,
        name="total",
    )(given, swap(own, "col"), bias_sum)
    sent = pl.pallas_call(
        join_kernel,
        out_shape=jax.ShapeDtypeStruct((chips, B + 3 * PART, B), jnp.bfloat16),
        in_specs=[SMEM] + [VMEM] * 3,
        out_specs=VMEM,
        compiler_params=PARAMS,
        name="join",
    )(core, kept, given, other_core(given))
    feature_grad, weight_grad, bias_grad = pl.pallas_call(
        final_kernel,
        out_shape=(
            jax.ShapeDtypeStruct((B, B), jnp.float32),
            jax.ShapeDtypeStruct((RELS, B, B), jnp.float32),
            jax.ShapeDtypeStruct((1, B), jnp.float32),
        ),
        in_specs=[VMEM],
        out_specs=(VMEM,) * 3,
        compiler_params=PARAMS,
        name="final",
    )(swap(sent, "row", same_core))
    return (activated, feature_grad, weight_grad, bias_grad.reshape(B))


def solution(mesh):
    placed = (
        P(("row", "col"), None),
        P("row", "col", None, None, None),
        P("row", "col", None),
        P("row", "col", None),
        P("row", "col", None),
        P("row", "col"),
        P(),
        P(),
        P(("row", "col"), None),
    )
    return jax.shard_map(
        on_device,
        mesh=mesh,
        in_specs=placed,
        out_specs=(P(("row", "col"), None), P(("row", "col"), None), P(), P()),
        check_vma=False,
    )
```

```python
import functools

import jax
import jax.numpy as jnp
from jax import lax
from jax.experimental import pallas as pl
from jax.experimental.pallas import tpu as pltpu
from jax.sharding import PartitionSpec as P

RB = 16
CB = 32
RELS = 4
B = 128
TILES = 96
BATCH = 4
SHORT = 16
CHUNK_BITS = 4
CHUNK = 1 << CHUNK_BITS
CHUNKS = TILES // CHUNK
SLICE = CB // RELS
PART = B // SLICE


def dot(a, b):
    return jnp.dot(a, b, preferred_element_type=jnp.float32)


def place(code):
    row, col, rel = code & (RB - 1), (code >> 4) & (CB - 1), (code >> 9) & (RELS - 1)
    return row, col, pl.multiple_of(rel * B, B)


def forward_kernel(
    which, ids, live, side, core, own_x, other_x, v, w, z, p, *rest
):
    lists = rest[0] if which == 0 else None
    x, acc, tiles, wide, listed, sems = rest[-6:]

    def chunk(g):
        span = pl.ds(g * CHUNK, CHUNK)
        return pltpu.make_async_copy(v.at[0, 0, span], tiles.at[span], sems.at[g])

    load_w = pltpu.make_async_copy(w.at[: RELS * B], wide, sems.at[CHUNKS])
    for g in range(CHUNKS):
        chunk(g).start()
    load_w.start()
    acc[...] = jnp.zeros_like(acc)
    x[0] = own_x[...]
    x[1] = other_x[...]
    mine = core[0, 0]
    wanted = side[0, 0] ^ which

    def put(k, at):
        code = ids[0, 0, k]
        listed[at] = code + (k << 11)
        return at + jnp.where((code & 1) == wanted, 1, 0)

    count = lax.fori_loop(0, live[0, 0], put, 0)
    for u in range(SHORT):
        listed[count + u] = 0

    def arrive(g, carry):
        chunk(g).wait()
        return carry

    def group(g, arrived):
        last = jnp.minimum(g * SHORT + SHORT, count) - 1
        needed = jnp.maximum((listed[last] >> (11 + CHUNK_BITS)) + 1, arrived)
        lax.fori_loop(arrived, needed, arrive, 0)
        for u in range(SHORT):
            i = g * SHORT + u
            code = listed[i]
            row, col, lane = place(code)
            product = dot(tiles[code >> 11], x[(col & 1) ^ mine, col >> 1])
            product = jnp.where(i < count, product, 0.0)
            acc[row >> 1, :, pl.ds(lane, B)] += product
        return needed

    arrived = lax.fori_loop(0, (count + SHORT - 1) // SHORT, group, 0)
    lax.fori_loop(arrived, CHUNKS, arrive, 0)
    load_w.wait()

    def finish(i, carry):
        rows = pl.ds(i * BATCH, BATCH)
        held = acc[rows].astype(jnp.bfloat16)
        p[rows] = held
        part = dot(held.reshape(BATCH * B, RELS * B), wide[...])
        z[rows] = part.astype(z.dtype).reshape(BATCH, B, B)
        return carry

    lax.fori_loop(0, RB // 2 // BATCH, finish, 0, unroll=2)
    if which == 0:
        both_lists(ids, live[0, 0], side[0, 0], lists)


def both_lists(ids, live, side, lists):
    def put(k, at):
        code = ids[0, 0, k]
        other = (code & 1) ^ side
        lists[other, jnp.where(other == 1, at, k - at)] = code + (k << 11)
        return at + other

    given = lax.fori_loop(0, live, put, 0)
    for u in range(SHORT):
        lists[0, live - given + u] = 0
        lists[1, given + u] = 0
    lists[0, TILES + SHORT] = live - given
    lists[1, TILES + SHORT] = given


def middle_kernel(parts, bias, out_grad, activated, grad_t):
    z = parts[0].astype(jnp.float32)
    for c in range(1, parts.shape[0]):
        z = z + parts[c].astype(jnp.float32)
    z = z + bias[...]
    s = jax.nn.sigmoid(z)
    activated[...] = (z * s).astype(jnp.bfloat16)
    slope = s * (1.0 + z * (1.0 - s))
    grad = (out_grad[...].astype(jnp.float32) * slope).astype(jnp.bfloat16)
    turned = grad.astype(jnp.float32).T.astype(jnp.bfloat16)
    for i in range(grad_t.shape[0]):
        grad_t[i] = turned


def early_kernel(lists, core, grad_t, p, v, w, total, bias_sum, acc, back):
    total[...] = jnp.zeros_like(total)
    bias_sum[...] = jnp.zeros_like(bias_sum)
    acc[...] = jnp.zeros_like(acc)
    weight_rows(grad_t, p, total, bias_sum)
    back_rows(grad_t, w[...], back)
    back_tiles(0, lists, core[0, 0], v, back, acc)


def back_tiles(which, lists, mine, v, back, acc):
    count = lists[which, TILES + SHORT]

    def group(g, carry):
        for u in range(SHORT):
            i = g * SHORT + u
            code = lists[which, i]
            row, col, at = place(code)
            product = dot(back[row >> 1, pl.ds(at, B), :], v[0, 0, code >> 11])
            product = jnp.where(i < count, product, 0.0)
            acc[(col & 1) ^ mine, col >> 1] += product
        return carry

    lax.fori_loop(0, (count + SHORT - 1) // SHORT, group, 0)


def weight_rows(grad_t, p, total, bias_sum):
    ones = jnp.ones((8, 2 * B), jnp.bfloat16)

    def add(i, carry):
        g = jnp.concatenate([grad_t[2 * i], grad_t[2 * i + 1]], axis=1)
        total[...] += dot(g, p[pl.ds(2 * i, 2)].reshape(2 * B, RELS * B))
        bias_sum[...] += lax.dot_general(
            ones, g, (((1,), (1,)), ((), ())), preferred_element_type=jnp.float32
        )
        return carry

    lax.fori_loop(0, RB // 4, add, 0, unroll=2)


def back_rows(grad_t, wide, back):
    def start(i, carry):
        g = jnp.concatenate([grad_t[2 * i], grad_t[2 * i + 1]], axis=1)
        both = dot(wide, g).astype(jnp.bfloat16)
        back[2 * i] = both[:, :B]
        back[2 * i + 1] = both[:, B:]
        return carry

    lax.fori_loop(0, RB // 4, start, 0, unroll=2)


def spread_kernel(parts, out):
    total = parts[0].astype(jnp.float32)
    for r in range(1, parts.shape[0]):
        total = total + parts[r].astype(jnp.float32)
    total = total.astype(jnp.bfloat16)
    for c in range(out.shape[0]):
        out[c] = total


def late_kernel(
    lists, core, grad_t, p, v, w, early_total, early_bias, early_acc,
    weight_parts, bias_sum, kept, given, total, back, acc
):
    total[...] = early_total[...]
    bias_sum[...] = early_bias[...]
    weight_rows(grad_t, p, total, bias_sum)
    for b in range(CB):
        rel, part = b // SLICE, b % SLICE
        term = total[part * PART : (part + 1) * PART, rel * B : (rel + 1) * B]
        weight_parts[b] = term.astype(jnp.bfloat16)
    acc[...] = early_acc[...]
    back_rows(grad_t, w[...], back)
    back_tiles(1, lists, core[0, 0], v, back, acc)
    kept[...] = acc[0].astype(jnp.bfloat16)
    given[: CB // 2] = acc[1].astype(jnp.bfloat16)
    given[CB // 2] = jnp.zeros((B, B), jnp.bfloat16)


def total_kernel(given, parts, bias_sum, out):
    total = parts[0].astype(jnp.float32)
    for c in range(1, parts.shape[0]):
        total = total + parts[c].astype(jnp.float32)
    row = lax.broadcasted_iota(jnp.int32, (PART, B), 0)
    term = jnp.broadcast_to(bias_sum[0:1, :], (PART, B))
    high = term.astype(jnp.bfloat16).astype(jnp.float32)
    pair = jnp.where(row == 0, high, jnp.where(row == 1, term - high, 0.0))
    out[CB // 2, : 2 * PART, :] = jnp.concatenate([total, pair], axis=0).astype(jnp.bfloat16)


def join_kernel(core, kept, given, taken, out):
    chips = out.shape[0]
    total = kept[...].astype(jnp.float32) + taken[:chips].astype(jnp.float32)
    out[:, :B, :] = total.astype(jnp.bfloat16)
    first = core[0, 0] == 0
    mine = given[chips, : 2 * PART, :].astype(jnp.float32)
    theirs = taken[chips, : 2 * PART, :].astype(jnp.float32)
    low = jnp.where(first, mine, theirs)
    high = jnp.where(first, theirs, mine)
    row = lax.broadcasted_iota(jnp.int32, (PART, B), 0)
    second = jnp.concatenate([high[PART + 8 :], high[PART : PART + 8]], axis=0)
    pair = jnp.where(row < 8, low[PART:], second)
    rows = jnp.concatenate([low[:PART], high[:PART], pair], axis=0).astype(jnp.bfloat16)
    for r in range(chips):
        out[r, B:, :] = rows


def final_kernel(received, feature_grad, weight_grad, bias_grad):
    total = received[0, :B].astype(jnp.float32)
    pair = received[0, B + 2 * PART :].astype(jnp.float32)
    for r in range(1, received.shape[0]):
        total = total + received[r, :B].astype(jnp.float32)
        pair = pair + received[r, B + 2 * PART :].astype(jnp.float32)
    feature_grad[...] = total.T
    bias_grad[...] = jnp.sum(pair, axis=0, keepdims=True)
    each = SLICE // 2
    for rel in range(RELS):
        parts = [received[rel * each + i, B : B + 2 * PART] for i in range(each)]
        weight_grad[rel] = jnp.concatenate(parts, axis=0).astype(jnp.float32).T


VMEM = pl.BlockSpec(memory_space=pltpu.VMEM)
SMEM = pl.BlockSpec(memory_space=pltpu.SMEM)
ANY = pl.BlockSpec(memory_space=pl.ANY)
WIDE = pltpu.CompilerParams(vmem_limit_bytes=50 * 1024 * 1024)
PARAMS = pltpu.CompilerParams(vmem_limit_bytes=32 * 1024 * 1024)


def swap(blocks, axis, groups=None):
    return lax.all_to_all(blocks, axis, 0, 0, tiled=True, axis_index_groups=groups)


def other_core(block):
    return lax.ppermute(block, "row", [(r, r ^ 1) for r in range(CB)])


def on_device(
    features, tile_values, tile_rows, tile_cols, tile_rels, live, weights, bias, out_grad
):
    ids = tile_rows + (tile_cols << 4) + (tile_rels << 9)
    wide_weights = weights.reshape(RELS * B, B)
    chips = CB // 2
    same_core = [[2 * chip + core for chip in range(chips)] for core in range(2)]
    core = jnp.reshape(lax.axis_index("row") & 1, (1, 1)).astype(jnp.int32)
    own_x = swap(jnp.broadcast_to(features[None], (chips, B, B)), "row", same_core)
    other_x = other_core(own_x)
    side = jnp.reshape(lax.axis_index("col") & 1, (1, 1)).astype(jnp.int32)

    early_weights = jnp.pad(wide_weights, ((0, PART), (0, 0)))

    def forward(which, z_type):
        return pl.pallas_call(
            functools.partial(forward_kernel, which),
            out_shape=(
                jax.ShapeDtypeStruct((RB // 2, B, B), z_type),
                jax.ShapeDtypeStruct((RB // 2, B, RELS * B), jnp.bfloat16),
            )
            + (jax.ShapeDtypeStruct((2, TILES + SHORT + 1), jnp.int32),) * (1 - which),
            in_specs=[SMEM] * 4 + [VMEM] * 2 + [ANY] * 2,
            out_specs=(VMEM, VMEM) + (SMEM,) * (1 - which),
            scratch_shapes=[
                pltpu.VMEM((2, chips, B, B), jnp.bfloat16),
                pltpu.VMEM((RB // 2, B, RELS * B), jnp.float32),
                pltpu.VMEM((TILES, B, B), jnp.bfloat16),
                pltpu.VMEM((RELS * B, B), jnp.bfloat16),
                pltpu.SMEM((TILES + SHORT,), jnp.int32),
                pltpu.SemaphoreType.DMA((CHUNKS + 1,)),
            ],
            compiler_params=WIDE,
            cost_estimate=pl.CostEstimate(flops=10**9, bytes_accessed=10**7, transcendentals=0),
            name="forward",
        )(ids, live, side, core, own_x, other_x, tile_values, early_weights)

    def partner(r, c):
        return c ^ 1 if r % 2 == 0 else ((c + 1) ^ 1) - 1

    pairs = [(r * RB + c, r * RB + partner(r, c) % RB) for r in range(CB) for c in range(RB)]
    z_other, p_other = forward(1, jnp.bfloat16)
    z_other = lax.ppermute(z_other, ("row", "col"), pairs)
    z_own, p_own, lists = forward(0, jnp.float32)
    z_parts = (z_own + z_other.astype(jnp.float32)).astype(jnp.bfloat16)
    same_side = [[2 * i + c for i in range(RB // 2)] for c in range(2)]
    activated, grad_t = pl.pallas_call(
        middle_kernel,
        out_shape=(
            jax.ShapeDtypeStruct((B, B), jnp.bfloat16),
            jax.ShapeDtypeStruct((RB // 2, B, B), jnp.bfloat16),
        ),
        in_specs=[VMEM] * 3,
        out_specs=(VMEM,) * 2,
        compiler_params=PARAMS,
        name="middle",
    )(swap(z_parts, "col", same_side), bias.reshape(1, B), out_grad)
    grad_own = swap(grad_t, "col", same_side)
    grad_other = lax.ppermute(grad_own, ("row", "col"), pairs)
    early_total, early_bias, early_acc = pl.pallas_call(
        early_kernel,
        out_shape=(
            jax.ShapeDtypeStruct((B, RELS * B), jnp.float32),
            jax.ShapeDtypeStruct((8, B), jnp.float32),
            jax.ShapeDtypeStruct((2, chips, B, B), jnp.float32),
        ),
        in_specs=[SMEM] * 2 + [VMEM] * 4,
        out_specs=(VMEM,) * 3,
        scratch_shapes=[pltpu.VMEM((RB // 2, RELS * B, B), jnp.bfloat16)],
        compiler_params=PARAMS,
        cost_estimate=pl.CostEstimate(flops=10**9, bytes_accessed=10**7, transcendentals=0),
        name="early",
    )(lists, core, grad_own, p_own, tile_values, wide_weights)
    weight_parts, bias_sum, kept, given = pl.pallas_call(
        late_kernel,
        out_shape=(
            jax.ShapeDtypeStruct((CB, PART, B), jnp.bfloat16),
            jax.ShapeDtypeStruct((8, B), jnp.float32),
            jax.ShapeDtypeStruct((chips, B, B), jnp.bfloat16),
            jax.ShapeDtypeStruct((chips + 1, B, B), jnp.bfloat16),
        ),
        in_specs=[SMEM] * 2 + [VMEM] * 7,
        out_specs=(VMEM,) * 4,
        scratch_shapes=[
            pltpu.VMEM((B, RELS * B), jnp.float32),
            pltpu.VMEM((RB // 2, RELS * B, B), jnp.bfloat16),
            pltpu.VMEM((2, chips, B, B), jnp.float32),
        ],
        compiler_params=PARAMS,
        name="late",
    )(lists, core, grad_other, p_other, tile_values, wide_weights, early_total, early_bias, early_acc)
    own = pl.pallas_call(
        spread_kernel,
        out_shape=jax.ShapeDtypeStruct((RB, PART, B), jnp.bfloat16),
        in_specs=[VMEM],
        out_specs=VMEM,
        compiler_params=PARAMS,
        name="spread",
    )(swap(weight_parts, "row"))
    given = pl.pallas_call(
        total_kernel,
        out_shape=jax.ShapeDtypeStruct(given.shape, given.dtype),
        in_specs=[VMEM] * 3,
        out_specs=VMEM,
        input_output_aliases={0: 0},
        compiler_params=PARAMS,
        name="total",
    )(given, swap(own, "col"), bias_sum)
    sent = pl.pallas_call(
        join_kernel,
        out_shape=jax.ShapeDtypeStruct((chips, B + 3 * PART, B), jnp.bfloat16),
        in_specs=[SMEM] + [VMEM] * 3,
        out_specs=VMEM,
        compiler_params=PARAMS,
        name="join",
    )(core, kept, given, other_core(given))
    feature_grad, weight_grad, bias_grad = pl.pallas_call(
        final_kernel,
        out_shape=(
            jax.ShapeDtypeStruct((B, B), jnp.float32),
            jax.ShapeDtypeStruct((RELS, B, B), jnp.float32),
            jax.ShapeDtypeStruct((1, B), jnp.float32),
        ),
        in_specs=[VMEM],
        out_specs=(VMEM,) * 3,
        compiler_params=PARAMS,
        name="final",
    )(swap(sent, "row", same_core))
    return (activated, feature_grad, weight_grad, bias_grad.reshape(B))


def solution(mesh):
    placed = (
        P(("row", "col"), None),
        P("row", "col", None, None, None),
        P("row", "col", None),
        P("row", "col", None),
        P("row", "col", None),
        P("row", "col"),
        P(),
        P(),
        P(("row", "col"), None),
    )
    return jax.shard_map(
        on_device,
        mesh=mesh,
        in_specs=placed,
        out_specs=(P(("row", "col"), None), P(("row", "col"), None), P(), P()),
        check_vma=False,
    )
```

```python
import functools

import jax
import jax.numpy as jnp
from jax import lax
from jax.experimental import pallas as pl
from jax.experimental.pallas import tpu as pltpu
from jax.sharding import PartitionSpec as P

RB = 16
CB = 32
RELS = 4
B = 128
TILES = 96
BATCH = 4
SHORT = 24
CHUNK_BITS = 4
CHUNK = 1 << CHUNK_BITS
CHUNKS = TILES // CHUNK
SLICE = CB // RELS
PART = B // SLICE


def dot(a, b):
    return jnp.dot(a, b, preferred_element_type=jnp.float32)


def place(code):
    row, col, rel = code & (RB - 1), (code >> 4) & (CB - 1), (code >> 9) & (RELS - 1)
    return row, col, pl.multiple_of(rel * B, B)


def forward_kernel(
    which, ids, side, core, own_x, other_x, v, w, z, p, *rest
):
    lists = rest[0] if which == 0 else None
    x, acc, tiles, wide, listed, sems = rest[-6:]

    def chunk(g):
        span = pl.ds(g * CHUNK, CHUNK)
        return pltpu.make_async_copy(v.at[0, 0, span], tiles.at[span], sems.at[g])

    load_w = pltpu.make_async_copy(w.at[: RELS * B], wide, sems.at[CHUNKS])
    for g in range(CHUNKS):
        chunk(g).start()
    load_w.start()
    acc[...] = jnp.zeros_like(acc)
    x[0] = own_x[...]
    x[1] = other_x[...]
    mine = core[0, 0]
    wanted = side[0, 0] ^ which

    def put(k, at):
        code = ids[0, 0, k] & ((1 << 11) - 1)
        listed[at] = code + (k << 11)
        return at + jnp.where((code & 1) == wanted, 1, 0)

    count = lax.fori_loop(0, ids[0, 0, 0] >> 11, put, 0)
    for u in range(SHORT):
        listed[count + u] = 0

    def arrive(g, carry):
        chunk(g).wait()
        return carry

    def group(g, arrived):
        last = jnp.minimum(g * SHORT + SHORT, count) - 1
        needed = jnp.maximum((listed[last] >> (11 + CHUNK_BITS)) + 1, arrived)
        lax.fori_loop(arrived, needed, arrive, 0)
        for u in range(SHORT):
            i = g * SHORT + u
            code = listed[i]
            row, col, lane = place(code)
            product = dot(tiles[code >> 11], x[(col & 1) ^ mine, col >> 1])
            product = jnp.where(i < count, product, 0.0)
            acc[row >> 1, :, pl.ds(lane, B)] += product
        return needed

    arrived = lax.fori_loop(0, (count + SHORT - 1) // SHORT, group, 0)
    lax.fori_loop(arrived, CHUNKS, arrive, 0)
    load_w.wait()

    def finish(i, carry):
        rows = pl.ds(i * BATCH, BATCH)
        held = acc[rows].astype(jnp.bfloat16)
        p[rows] = held
        part = dot(held.reshape(BATCH * B, RELS * B), wide[...])
        z[rows] = part.astype(z.dtype).reshape(BATCH, B, B)
        return carry

    lax.fori_loop(0, RB // 2 // BATCH, finish, 0, unroll=2)
    if which == 0:
        both_lists(ids, ids[0, 0, 0] >> 11, side[0, 0], lists)


def both_lists(ids, live, side, lists):
    def put(k, at):
        code = ids[0, 0, k] & ((1 << 11) - 1)
        other = (code & 1) ^ side
        lists[other, jnp.where(other == 1, at, k - at)] = code + (k << 11)
        return at + other

    given = lax.fori_loop(0, live, put, 0)
    for u in range(SHORT):
        lists[0, live - given + u] = 0
        lists[1, given + u] = 0
    lists[0, TILES + SHORT] = live - given
    lists[1, TILES + SHORT] = given


def middle_kernel(parts, bias, out_grad, activated, grad_t):
    z = parts[0].astype(jnp.float32)
    for c in range(1, parts.shape[0]):
        z = z + parts[c].astype(jnp.float32)
    z = z + bias[...]
    s = jax.nn.sigmoid(z)
    activated[...] = (z * s).astype(jnp.bfloat16)
    slope = s * (1.0 + z * (1.0 - s))
    grad = (out_grad[...].astype(jnp.float32) * slope).astype(jnp.bfloat16)
    turned = grad.astype(jnp.float32).T.astype(jnp.bfloat16)
    for i in range(grad_t.shape[0]):
        grad_t[i] = turned


def early_kernel(lists, core, grad_t, p, v, w, total, bias_sum, acc, back):
    total[...] = jnp.zeros_like(total)
    bias_sum[...] = jnp.zeros_like(bias_sum)
    acc[...] = jnp.zeros_like(acc)
    weight_rows(grad_t, p, total, bias_sum)
    back_rows(grad_t, w[...], back)
    back_tiles(0, lists, core[0, 0], v, back, acc)


def back_tiles(which, lists, mine, v, back, acc):
    count = lists[which, TILES + SHORT]

    def group(g, carry):
        for u in range(SHORT):
            i = g * SHORT + u
            code = lists[which, i]
            row, col, at = place(code)
            product = dot(back[row >> 1, pl.ds(at, B), :], v[0, 0, code >> 11])
            product = jnp.where(i < count, product, 0.0)
            acc[(col & 1) ^ mine, col >> 1] += product
        return carry

    lax.fori_loop(0, (count + SHORT - 1) // SHORT, group, 0)


def weight_rows(grad_t, p, total, bias_sum):
    ones = jnp.ones((8, 2 * B), jnp.bfloat16)

    def add(i, carry):
        g = jnp.concatenate([grad_t[2 * i], grad_t[2 * i + 1]], axis=1)
        total[...] += dot(g, p[pl.ds(2 * i, 2)].reshape(2 * B, RELS * B))
        bias_sum[...] += lax.dot_general(
            ones, g, (((1,), (1,)), ((), ())), preferred_element_type=jnp.float32
        )
        return carry

    lax.fori_loop(0, RB // 4, add, 0, unroll=2)


def back_rows(grad_t, wide, back):
    def start(i, carry):
        g = jnp.concatenate([grad_t[2 * i], grad_t[2 * i + 1]], axis=1)
        both = dot(wide, g).astype(jnp.bfloat16)
        back[2 * i] = both[:, :B]
        back[2 * i + 1] = both[:, B:]
        return carry

    lax.fori_loop(0, RB // 4, start, 0, unroll=2)


def spread_kernel(parts, out):
    total = parts[0].astype(jnp.float32)
    for r in range(1, parts.shape[0]):
        total = total + parts[r].astype(jnp.float32)
    total = total.astype(jnp.bfloat16)
    for c in range(out.shape[0]):
        out[c] = total


def late_kernel(
    lists, core, grad_t, p, v, w, early_total, early_bias, early_acc,
    weight_parts, bias_sum, kept, given, total, back, acc
):
    total[...] = early_total[...]
    bias_sum[...] = early_bias[...]
    weight_rows(grad_t, p, total, bias_sum)
    for b in range(CB):
        rel, part = b // SLICE, b % SLICE
        term = total[part * PART : (part + 1) * PART, rel * B : (rel + 1) * B]
        weight_parts[b] = term.astype(jnp.bfloat16)
    acc[...] = early_acc[...]
    back_rows(grad_t, w[...], back)
    back_tiles(1, lists, core[0, 0], v, back, acc)
    kept[...] = acc[0].astype(jnp.bfloat16)
    given[: CB // 2] = acc[1].astype(jnp.bfloat16)
    given[CB // 2] = jnp.zeros((B, B), jnp.bfloat16)


def total_kernel(given, parts, bias_sum, out):
    total = parts[0].astype(jnp.float32)
    for c in range(1, parts.shape[0]):
        total = total + parts[c].astype(jnp.float32)
    row = lax.broadcasted_iota(jnp.int32, (PART, B), 0)
    term = jnp.broadcast_to(bias_sum[0:1, :], (PART, B))
    high = term.astype(jnp.bfloat16).astype(jnp.float32)
    pair = jnp.where(row == 0, high, jnp.where(row == 1, term - high, 0.0))
    out[CB // 2, : 2 * PART, :] = jnp.concatenate([total, pair], axis=0).astype(jnp.bfloat16)


def join_kernel(core, kept, given, taken, out):
    chips = out.shape[0]
    total = kept[...].astype(jnp.float32) + taken[:chips].astype(jnp.float32)
    out[:, :B, :] = total.astype(jnp.bfloat16)
    first = core[0, 0] == 0
    mine = given[chips, : 2 * PART, :].astype(jnp.float32)
    theirs = taken[chips, : 2 * PART, :].astype(jnp.float32)
    low = jnp.where(first, mine, theirs)
    high = jnp.where(first, theirs, mine)
    row = lax.broadcasted_iota(jnp.int32, (PART, B), 0)
    second = jnp.concatenate([high[PART + 8 :], high[PART : PART + 8]], axis=0)
    pair = jnp.where(row < 8, low[PART:], second)
    rows = jnp.concatenate([low[:PART], high[:PART], pair], axis=0).astype(jnp.bfloat16)
    for r in range(chips):
        out[r, B:, :] = rows


def final_kernel(received, feature_grad, weight_grad, bias_grad):
    total = received[0, :B].astype(jnp.float32)
    pair = received[0, B + 2 * PART :].astype(jnp.float32)
    for r in range(1, received.shape[0]):
        total = total + received[r, :B].astype(jnp.float32)
        pair = pair + received[r, B + 2 * PART :].astype(jnp.float32)
    feature_grad[...] = total.T
    bias_grad[...] = jnp.sum(pair, axis=0, keepdims=True)
    each = SLICE // 2
    for rel in range(RELS):
        parts = [received[rel * each + i, B : B + 2 * PART] for i in range(each)]
        weight_grad[rel] = jnp.concatenate(parts, axis=0).astype(jnp.float32).T


VMEM = pl.BlockSpec(memory_space=pltpu.VMEM)
SMEM = pl.BlockSpec(memory_space=pltpu.SMEM)
ANY = pl.BlockSpec(memory_space=pl.ANY)
WIDE = pltpu.CompilerParams(vmem_limit_bytes=50 * 1024 * 1024)
PARAMS = pltpu.CompilerParams(vmem_limit_bytes=32 * 1024 * 1024)


def swap(blocks, axis, groups=None):
    return lax.all_to_all(blocks, axis, 0, 0, tiled=True, axis_index_groups=groups)


def other_core(block):
    return lax.ppermute(block, "row", [(r, r ^ 1) for r in range(CB)])


def on_device(
    features, tile_values, tile_rows, tile_cols, tile_rels, live, weights, bias, out_grad
):
    ids = tile_rows + (tile_cols << 4) + (tile_rels << 9) + (live.reshape(1, 1, 1) << 11)
    wide_weights = weights.reshape(RELS * B, B)
    chips = CB // 2
    same_core = [[2 * chip + core for chip in range(chips)] for core in range(2)]
    core = jnp.reshape(lax.axis_index("row") & 1, (1, 1)).astype(jnp.int32)
    own_x = swap(jnp.broadcast_to(features[None], (chips, B, B)), "row", same_core)
    other_x = other_core(own_x)
    side = jnp.reshape(lax.axis_index("col") & 1, (1, 1)).astype(jnp.int32)

    early_weights = jnp.pad(wide_weights, ((0, PART), (0, 0)))

    def forward(which, z_type):
        return pl.pallas_call(
            functools.partial(forward_kernel, which),
            out_shape=(
                jax.ShapeDtypeStruct((RB // 2, B, B), z_type),
                jax.ShapeDtypeStruct((RB // 2, B, RELS * B), jnp.bfloat16),
            )
            + (jax.ShapeDtypeStruct((2, TILES + SHORT + 1), jnp.int32),) * (1 - which),
            in_specs=[SMEM] * 3 + [VMEM] * 2 + [ANY] * 2,
            out_specs=(VMEM, VMEM) + (SMEM,) * (1 - which),
            scratch_shapes=[
                pltpu.VMEM((2, chips, B, B), jnp.bfloat16),
                pltpu.VMEM((RB // 2, B, RELS * B), jnp.float32),
                pltpu.VMEM((TILES, B, B), jnp.bfloat16),
                pltpu.VMEM((RELS * B, B), jnp.bfloat16),
                pltpu.SMEM((TILES + SHORT,), jnp.int32),
                pltpu.SemaphoreType.DMA((CHUNKS + 1,)),
            ],
            compiler_params=WIDE,
            cost_estimate=pl.CostEstimate(flops=10**9, bytes_accessed=10**7, transcendentals=0),
            name="forward",
        )(ids, side, core, own_x, other_x, tile_values, early_weights)

    def partner(r, c):
        return c ^ 1 if r % 2 == 0 else ((c + 1) ^ 1) - 1

    pairs = [(r * RB + c, r * RB + partner(r, c) % RB) for r in range(CB) for c in range(RB)]
    z_other, p_other = forward(1, jnp.bfloat16)
    z_other = lax.ppermute(z_other, ("row", "col"), pairs)
    z_own, p_own, lists = forward(0, jnp.float32)
    z_parts = (z_own + z_other.astype(jnp.float32)).astype(jnp.bfloat16)
    same_side = [[2 * i + c for i in range(RB // 2)] for c in range(2)]
    activated, grad_t = pl.pallas_call(
        middle_kernel,
        out_shape=(
            jax.ShapeDtypeStruct((B, B), jnp.bfloat16),
            jax.ShapeDtypeStruct((RB // 2, B, B), jnp.bfloat16),
        ),
        in_specs=[VMEM] * 3,
        out_specs=(VMEM,) * 2,
        compiler_params=PARAMS,
        name="middle",
    )(swap(z_parts, "col", same_side), bias.reshape(1, B), out_grad)
    grad_own = swap(grad_t, "col", same_side)
    grad_other = lax.ppermute(grad_own, ("row", "col"), pairs)
    early_total, early_bias, early_acc = pl.pallas_call(
        early_kernel,
        out_shape=(
            jax.ShapeDtypeStruct((B, RELS * B), jnp.float32),
            jax.ShapeDtypeStruct((8, B), jnp.float32),
            jax.ShapeDtypeStruct((2, chips, B, B), jnp.float32),
        ),
        in_specs=[SMEM] * 2 + [VMEM] * 4,
        out_specs=(VMEM,) * 3,
        scratch_shapes=[pltpu.VMEM((RB // 2, RELS * B, B), jnp.bfloat16)],
        compiler_params=PARAMS,
        cost_estimate=pl.CostEstimate(flops=10**9, bytes_accessed=10**7, transcendentals=0),
        name="early",
    )(lists, core, grad_own, p_own, tile_values, wide_weights)
    weight_parts, bias_sum, kept, given = pl.pallas_call(
        late_kernel,
        out_shape=(
            jax.ShapeDtypeStruct((CB, PART, B), jnp.bfloat16),
            jax.ShapeDtypeStruct((8, B), jnp.float32),
            jax.ShapeDtypeStruct((chips, B, B), jnp.bfloat16),
            jax.ShapeDtypeStruct((chips + 1, B, B), jnp.bfloat16),
        ),
        in_specs=[SMEM] * 2 + [VMEM] * 7,
        out_specs=(VMEM,) * 4,
        scratch_shapes=[
            pltpu.VMEM((B, RELS * B), jnp.float32),
            pltpu.VMEM((RB // 2, RELS * B, B), jnp.bfloat16),
            pltpu.VMEM((2, chips, B, B), jnp.float32),
        ],
        compiler_params=PARAMS,
        name="late",
    )(lists, core, grad_other, p_other, tile_values, wide_weights, early_total, early_bias, early_acc)
    own = pl.pallas_call(
        spread_kernel,
        out_shape=jax.ShapeDtypeStruct((RB, PART, B), jnp.bfloat16),
        in_specs=[VMEM],
        out_specs=VMEM,
        compiler_params=PARAMS,
        name="spread",
    )(swap(weight_parts, "row"))
    given = pl.pallas_call(
        total_kernel,
        out_shape=jax.ShapeDtypeStruct(given.shape, given.dtype),
        in_specs=[VMEM] * 3,
        out_specs=VMEM,
        input_output_aliases={0: 0},
        compiler_params=PARAMS,
        name="total",
    )(given, swap(own, "col"), bias_sum)
    sent = pl.pallas_call(
        join_kernel,
        out_shape=jax.ShapeDtypeStruct((chips, B + 3 * PART, B), jnp.bfloat16),
        in_specs=[SMEM] + [VMEM] * 3,
        out_specs=VMEM,
        compiler_params=PARAMS,
        name="join",
    )(core, kept, given, other_core(given))
    feature_grad, weight_grad, bias_grad = pl.pallas_call(
        final_kernel,
        out_shape=(
            jax.ShapeDtypeStruct((B, B), jnp.float32),
            jax.ShapeDtypeStruct((RELS, B, B), jnp.float32),
            jax.ShapeDtypeStruct((1, B), jnp.float32),
        ),
        in_specs=[VMEM],
        out_specs=(VMEM,) * 3,
        compiler_params=PARAMS,
        name="final",
    )(swap(sent, "row", same_core))
    return (activated, feature_grad, weight_grad, bias_grad.reshape(B))


def solution(mesh):
    placed = (
        P(("row", "col"), None),
        P("row", "col", None, None, None),
        P("row", "col", None),
        P("row", "col", None),
        P("row", "col", None),
        P("row", "col"),
        P(),
        P(),
        P(("row", "col"), None),
    )
    return jax.shard_map(
        on_device,
        mesh=mesh,
        in_specs=placed,
        out_specs=(P(("row", "col"), None), P(("row", "col"), None), P(), P()),
        check_vma=False,
    )
```
